32 devices in a mesh: groups: 2 (over y), rowblk: 4 (over x, core), colblk: 4 (over z).
Axes of the slice: x: 2, y: 2, z: 4, core: 2. Of those that a mesh axis runs over, the one named last changes fastest.
Arguments:
- tiles: bfloat16 [3072, 128, 128], P(('groups', 'rowblk', 'colblk')), parts along dimension 0, may hold values from -0.1875 to 0.1875
- tile_row: int32 [3072], P(('groups', 'rowblk', 'colblk')), parts along dimension 0, may hold values from 0 to 31, as said below
- tile_col: int32 [3072], P(('groups', 'rowblk', 'colblk')), parts along dimension 0, may hold values from 0 to 63
- tile_count: int32 [32], P(('groups', 'rowblk', 'colblk')), parts along dimension 0, may hold values from 12 to 96, as said below
- cost: float32 [65536], P(('groups', 'colblk')), parts along dimension 0, may hold values from -12 to 12
- demand: float32 [8, 32768], P(None, ('groups', 'rowblk')), parts along dimension 1, may hold values from -12 to 12
- upper: float32 [65536], P(('groups', 'colblk')), parts along dimension 0, may hold values from 0.5 to 2
- col_flag: int32 [65536], P(('groups', 'colblk')), parts along dimension 0, may hold values 0 or 1
- row_flag: int32 [32768], P(('groups', 'rowblk')), parts along dimension 0, may hold values 0 or 1
- primal_start: float32 [8, 65536], P(None, ('groups', 'colblk')), parts along dimension 1, may hold values from 0 to 1
- dual_start: float32 [8, 32768], P(None, ('groups', 'rowblk')), parts along dimension 1, may hold values from -3 to 3
Outputs:
- primal_point: float32 [8, 65536], P(None, ('groups', 'colblk')), parts along dimension 1
- dual_point: float32 [8, 32768], P(None, ('groups', 'rowblk')), parts along dimension 1
- primal_weight: float32 [16], P('groups'), parts along dimension 0
The draws below stay inside these ranges and needn't reach their ends.
There are 2 independent parts, one for each index of `groups`. The reference program is written for one: setup_inputs(seed, part) draws one part's arguments, and reference() takes and returns one part's arrays. A program takes and returns all parts, laid end to end along the dimension named above; each array names one. Nothing has to cross between parts.
Inputs may be any that keep to these rules, and one draw needn't show every extreme that they name: On one device the pairs (tile_row, tile_col) of its 96 slots are all different. `tile_count`: in every draw one device has all 96 slots live.
All inputs are finite; a program needn't handle non-finite values. No bound on the sum of `col_flag` or of `row_flag` on one device may be relied on, other than what follows from the above.
Results may differ from the reference program's by a relative error of at most 0.0012.
Values may be sent and summed in bfloat16 or wider, within the bound.
No kernel may reach another device: no remote copies, remote signals or barrier semaphores. Data moves between devices by JAX's collectives and lax.ppermute only.
A program may use at most 64 MiB of HBM per device.

```python
import math
import jax
import jax.numpy as jnp
from jax import lax

TILE = 128
RB_DEV = 32
CB_DEV = 64
TILES_DEV = 96
SCEN = 8
ITERS = 2
ROWS = 16384
COLS = 32768
SLOTS = 1536
N_ROWBLK = 4
N_COLBLK = 4


def pattern_slots(key):
    devices = N_ROWBLK * N_COLBLK

    def single(index):
        order = jax.random.permutation(jax.random.fold_in(key, index), RB_DEV * CB_DEV)
        return order[:TILES_DEV]
    picks = jax.vmap(single)(jnp.arange(devices, dtype=jnp.int32))
    return picks.reshape(-1).astype(jnp.int32)


def draw_tile_row(key, part):
    picks = pattern_slots(key)
    return (picks // CB_DEV).astype(jnp.int32)


def draw_tile_col(key, part):
    picks = pattern_slots(key)
    return (picks % CB_DEV).astype(jnp.int32)


def draw_tile_count(key, part):
    key = jax.random.fold_in(key, 3)
    devices = N_ROWBLK * N_COLBLK
    lower = jax.random.randint(jax.random.fold_in(key, 1), (devices,), TILES_DEV // 8, TILES_DEV // 2 + 1)
    busiest = jax.random.randint(jax.random.fold_in(key, 2), (), 0, devices)
    places = jnp.arange(devices, dtype=jnp.int32)
    return jnp.where(places == busiest, TILES_DEV, lower).astype(jnp.int32)


def ramped(key, shape, length):
    ramp = 1.0 + 2.0 * jnp.arange(length, dtype=jnp.float32) / length
    base = jnp.clip(jax.random.normal(key, shape, jnp.float32), -4.0, 4.0)
    return base * ramp


def draw_cost(key, part):
    key = jax.random.fold_in(key, 5)
    return ramped(key, (COLS,), COLS).astype(jnp.float32)


def draw_demand(key, part):
    key = jax.random.fold_in(key, 7)
    return ramped(key, (SCEN, ROWS), ROWS).astype(jnp.float32)


def touch_ends(drawn, own_key, low, largest):
    longest = drawn.shape.index(max(drawn.shape))
    spots = []
    for shift in (0, 1):
        where = [jax.random.randint(jax.random.fold_in(own_key, axis), (), 0, length) for axis, length in enumerate(drawn.shape)]
        where[longest] = (where[longest] + shift) % drawn.shape[longest]
        spots.append(tuple(where))
    return drawn.at[spots[0]].set(low).at[spots[1]].set(largest)


def steps_of(stream_key, shape, cuts, least, top_value):
    loudness = 1.0
    for dim, shards_of in cuts:
        heights = jax.random.uniform(jax.random.fold_in(jax.random.fold_in(stream_key, 6), dim), (shards_of,), jnp.float32, least / len(cuts), top_value / len(cuts))
        loudness = loudness * jnp.repeat(jnp.exp(heights), shape[dim] // shards_of).reshape((-1,) + (1,) * (len(shape) - 1 - dim))
    return loudness


def centred(own_key, extent, deviation, reach, pieces=(), kind=jnp.bfloat16):
    level = steps_of(own_key, extent, pieces, -0.22, 0.18) if pieces else 1.0
    values = jax.random.normal(own_key, extent, jnp.float32) * deviation * level
    return jnp.minimum(jnp.maximum(values, -reach), reach).astype(kind)


def setup_inputs(seed: int = 0, part: int = 0) -> dict:
    arg_keys = jax.random.split(jax.random.key(seed), 12)
    part_splits = jax.random.split(jax.random.fold_in(arg_keys[11], part), 12)
    tiles = centred(part_splits[0], (SLOTS, TILE, TILE), (8 * TILE) ** -0.5, 0.1875, ((0, 16),))
    tile_row = draw_tile_row(jax.random.fold_in(jax.random.fold_in(arg_keys[11], part), 71), part)
    tile_col = draw_tile_col(jax.random.fold_in(jax.random.fold_in(arg_keys[11], part), 71), part)
    tile_count = draw_tile_count(jax.random.fold_in(jax.random.fold_in(arg_keys[11], part), 71), part)
    cost = draw_cost(jax.random.fold_in(jax.random.fold_in(arg_keys[11], part), 71), part)
    demand = draw_demand(jax.random.fold_in(jax.random.fold_in(arg_keys[11], part), 71), part)
    upper = jnp.clip(jnp.exp(math.log(2.0) - 1.3862944 * jax.random.uniform(part_splits[6], (COLS,), jnp.float32) ** steps_of(part_splits[6], (COLS,), ((0, 4),), -0.2, 0.2)), 0.5, 2.0)
    col_flag = touch_ends((jax.random.randint(part_splits[7], (COLS,), 0, 2) < 1).astype(jnp.int32), jax.random.fold_in(part_splits[7], 1), 0, 1)
    row_flag = touch_ends((jax.random.randint(part_splits[8], (ROWS,), 0, 2) < 1).astype(jnp.int32), jax.random.fold_in(part_splits[8], 1), 0, 1)
    primal_start = jnp.clip(1.0 * jax.random.uniform(part_splits[9], (SCEN, COLS), jnp.float32) ** steps_of(part_splits[9], (SCEN, COLS), ((1, 4),), -0.2, 0.2), 0.0, 1.0)
    dual_start = centred(part_splits[10], (SCEN, ROWS), 0.5, 3.0, ((1, 4),), jnp.float32)
    return dict(tiles=tiles, tile_row=tile_row, tile_col=tile_col, tile_count=tile_count, cost=cost, demand=demand, upper=upper, col_flag=col_flag, row_flag=row_flag, primal_start=primal_start, dual_start=dual_start)


ETA = 0.3
EPS = 1e-06

def slot_layout(tile_row, tile_col, tile_count):
    slots = jnp.arange(tile_row.shape[0], dtype=jnp.int32)
    device = slots // TILES_DEV
    live = slots % TILES_DEV < tile_count[device]
    grow = device // N_COLBLK * RB_DEV + tile_row
    gcol = device % N_COLBLK * CB_DEV + tile_col
    return (live, grow.astype(jnp.int32), gcol.astype(jnp.int32))

def matrix_pass(tiles, live, grow, gcol, vector, out_len, backward):
    devices = tiles.shape[0] // TILES_DEV
    blocks = vector.reshape(SCEN, vector.shape[1] // TILE, TILE)
    items = (tiles.reshape(devices, TILES_DEV, TILE, TILE), live.reshape(devices, TILES_DEV), grow.reshape(devices, TILES_DEV), gcol.reshape(devices, TILES_DEV))

    def advance(acc, item):
        block, alive, rows, cols = item
        matrix = block.astype(jnp.float32)
        weight = alive.astype(jnp.float32)[None, :, None]
        if backward:
            picked = blocks[:, rows, :]
            contrib = jnp.einsum('gij,sgi->sgj', matrix, picked, precision=lax.Precision.HIGHEST) * weight
            acc = acc.at[:, cols, :].add(contrib)
        else:
            picked = blocks[:, cols, :]
            contrib = jnp.einsum('gij,sgj->sgi', matrix, picked, precision=lax.Precision.HIGHEST) * weight
            acc = acc.at[:, rows, :].add(contrib)
        return (acc, None)
    init = jnp.zeros((SCEN, out_len // TILE, TILE), jnp.float32)
    acc, _ = lax.scan(advance, init, items)
    return acc.reshape(SCEN, out_len)

def project_primal(point, partial_value, cost, upper, bounded, tau):
    moved = point - tau * (cost[None, :] - partial_value)
    moved = jnp.where(bounded[None, :], jnp.minimum(moved, upper[None, :]), moved)
    return jnp.maximum(moved, 0.0)

def reference(tiles, tile_row, tile_col, tile_count, cost, demand, upper, col_flag, row_flag, primal_start, dual_start):
    live, grow, gcol = slot_layout(tile_row, tile_col, tile_count)
    bounded = col_flag > 0
    inequal = row_flag > 0
    point, dual = (primal_start, dual_start)
    weight = jnp.ones((SCEN,), jnp.float32)
    for step in range(ITERS):
        tau = (ETA / weight)[:, None]
        sigma = (ETA * weight)[:, None]
        partial_value = matrix_pass(tiles, live, grow, gcol, dual, COLS, True)
        x_hat = project_primal(point, partial_value, cost, upper, bounded, tau)
        x_bar = 2.0 * x_hat - point
        summed = matrix_pass(tiles, live, grow, gcol, x_bar, ROWS, False)
        moved = dual + sigma * (demand - summed)
        y_hat = jnp.where(inequal[None, :], jnp.maximum(moved, 0.0), moved)
        primal_diff = x_hat - point
        dual_diff = y_hat - dual
        primal_norm = lax.optimization_barrier(jnp.sum(primal_diff * primal_diff, axis=1))
        dual_norm = lax.optimization_barrier(jnp.sum(dual_diff * dual_diff, axis=1))
        weight = jnp.sqrt(weight * jnp.sqrt((dual_norm + EPS) / (primal_norm + EPS)))
        mix = (step + 1.0) / (step + 2.0)
        point = mix * x_bar + (1.0 - mix) * primal_start
        dual = mix * (2.0 * y_hat - dual) + (1.0 - mix) * dual_start
    return (point, dual, weight)
```

```python
import functools

import jax
import jax.numpy as jnp
from jax import lax
from jax.experimental import pallas as pl
from jax.experimental.pallas import tpu as pltpu
from jax.sharding import PartitionSpec as P

ITERS = 2
ETA = 0.3
EPS = 1e-06
PART = 32
VMEM_LIMIT = 40 * 1024 * 1024

SMEM_SPEC = pl.BlockSpec(memory_space=pltpu.SMEM)
VMEM_SPEC = pl.BlockSpec(memory_space=pltpu.VMEM)


def split_rows(value):
    high = value.astype(jnp.bfloat16)
    low = (value - high.astype(jnp.float32)).astype(jnp.bfloat16)
    return jnp.concatenate([high, low], axis=0)


def join_rows(value):
    half = value.shape[0] // 2
    return value[:half].astype(jnp.float32) + value[half:].astype(jnp.float32)


def tile_products(count, rows, cols, tiles, source, acc, backward):
    total, tile = tiles.shape[0], tiles.shape[1]
    spare = acc.shape[0] - 1
    scen = acc.shape[1]
    live = count[0]
    depth = 0 if backward else 1
    dims = (((1,), (depth,)), ((), ()))
    acc[...] = jnp.zeros_like(acc)

    def part(first, size):
        landing, results = [], []
        for g in range(first, first + size):
            goes = cols[g] if backward else rows[g]
            landing.append(jnp.where(g < live, goes, spare))
        pair = 2 if size % 2 == 0 else 1
        for g in range(first, first + size, pair):
            picked = [source[rows[g + k] if backward else cols[g + k]] for k in range(pair)]
            if pair == 2:
                blank = jnp.zeros_like(picked[0])
                left = jnp.concatenate(
                    [
                        jnp.concatenate([picked[0], blank], axis=1),
                        jnp.concatenate([blank, picked[1]], axis=1),
                    ],
                    axis=0,
                )
                right = jnp.concatenate([tiles[g], tiles[g + 1]], axis=depth)
            else:
                left, right = picked[0], tiles[g]
            product = lax.dot_general(left, right, dims, preferred_element_type=jnp.float32)
            for k in range(pair):
                own = product[2 * scen * k : 2 * scen * (k + 1)]
                results.append(own[:scen] + own[scen:])
        for where, value in zip(landing, results):
            acc[where] += value

    for first in range(0, total, PART):
        size = min(PART, total - first)
        if first == 0:
            part(first, size)
        else:
            pl.when(first < live)(functools.partial(part, first, size))


def pack(acc, out, norm, slot):
    half = (acc.shape[0] - 1) // 2
    for b in range(half):
        out[b] = jnp.concatenate([acc[b], acc[b + half]], axis=0).astype(jnp.bfloat16)
    lanes = lax.broadcasted_iota(jnp.int32, (acc.shape[1], acc.shape[2]), 1)
    out[half] = split_rows(jnp.where(lanes == slot, norm, 0.0))


def unpack(parts, b, half):
    scen = parts[0].shape[1] // 2
    rows = slice(0, scen) if b < half else slice(scen, 2 * scen)
    k = b if b < half else b - half
    terms = [p[k, rows, :].astype(jnp.float32) for p in parts]
    while len(terms) > 1:
        terms = [terms[i] + terms[i + 1] for i in range(0, len(terms), 2)]
    return terms[0]


def unpack_norm(parts, half):
    terms = [join_rows(p[half]) for p in parts]
    while len(terms) > 1:
        terms = [terms[i] + terms[i + 1] for i in range(0, len(terms), 2)]
    return jnp.sum(terms[0], axis=1, keepdims=True)


def first_kernel(count, rows, cols, tiles, dual, out, source, acc):
    tile = tiles.shape[1]
    for b in range(source.shape[0]):
        source[b] = split_rows(dual[:, b * tile : (b + 1) * tile])
    tile_products(count, rows, cols, tiles, source, acc, True)
    pack(acc, out, 0.0, 0)


def primal_kernel(mix, n_parts, *refs):
    count, rows, cols, slot, tiles = refs[:5]
    parts = refs[5 : 5 + n_parts]
    refs = refs[5 + n_parts :]
    weight_in, primal_norm, cost, upper, flag, point, start = refs[:7]
    point_out, weight_out, out, source, acc = refs[7:]
    tile = tiles.shape[1]
    blocks = source.shape[0]
    half = blocks // 2
    if mix > 0.5:
        dual_norm = unpack_norm(parts, half)
        weight = weight_in[:, :1]
        ratio = (dual_norm + EPS) / (primal_norm[:, :1] + EPS)
        weight = jnp.sqrt(weight * jnp.sqrt(ratio))
        weight_out[...] = jnp.broadcast_to(weight, weight_out.shape)
        tau = ETA / weight
    else:
        weight_out[...] = weight_in[...]
        tau = ETA / weight_in[:, :1]
    tau = jnp.broadcast_to(tau, (tau.shape[0], tile))
    moved_norm = jnp.zeros_like(tau)
    for b in range(blocks):
        lanes = slice(b * tile, (b + 1) * tile)
        value = unpack(parts, b, half)
        old = point[:, lanes]
        moved = old - tau * (cost[b : b + 1, :] - value)
        limit = jnp.where(flag[b : b + 1, :] > 0, upper[b : b + 1, :], jnp.inf)
        x_hat = jnp.maximum(jnp.minimum(moved, limit), 0.0)
        step = x_hat - old
        moved_norm += step * step
        x_bar = 2.0 * x_hat - old
        point_out[:, lanes] = mix * x_bar + (1.0 - mix) * start[:, lanes]
        source[b] = split_rows(x_bar)
    tile_products(count, rows, cols, tiles, source, acc, False)
    pack(acc, out, jnp.sum(moved_norm, axis=1, keepdims=True), slot[0])


def dual_kernel(mix, last, n_parts, *refs):
    count, rows, cols, slot, tiles = refs[:5]
    parts = refs[5 : 5 + n_parts]
    refs = refs[5 + n_parts :]
    weight, demand, flag, dual, start = refs[:5]
    if last:
        dual_out, primal_norm, out = refs[5:]
    else:
        dual_out, primal_norm, out, source, acc = refs[5:]
    tile = flag.shape[1]
    blocks = flag.shape[0]
    half = blocks // 2
    primal_norm[...] = jnp.broadcast_to(unpack_norm(parts, half), primal_norm.shape)
    sigma = ETA * weight[...]
    moved_norm = jnp.zeros_like(sigma)
    for b in range(blocks):
        lanes = slice(b * tile, (b + 1) * tile)
        value = unpack(parts, b, half)
        old = dual[:, lanes]
        moved = old + sigma * (demand[:, lanes] - value)
        floor = jnp.where(flag[b : b + 1, :] > 0, 0.0, -jnp.inf)
        y_hat = jnp.maximum(moved, floor)
        step = y_hat - old
        moved_norm += step * step
        new = mix * (2.0 * y_hat - old) + (1.0 - mix) * start[:, lanes]
        dual_out[:, lanes] = new
        if not last:
            source[b] = split_rows(new)
    dual_norm = jnp.sum(moved_norm, axis=1, keepdims=True)
    if last:
        lanes = lax.broadcasted_iota(jnp.int32, out.shape, 1)
        out[...] = jnp.where(lanes == slot[0], dual_norm, 0.0)
    else:
        tile_products(count, rows, cols, tiles, source, acc, True)
        pack(acc, out, dual_norm, slot[0])


def call(kernel, inputs, outputs, scratch, scalars):
    specs = [SMEM_SPEC] * scalars + [VMEM_SPEC] * (len(inputs) - scalars)
    return pl.pallas_call(
        kernel,
        out_shape=outputs,
        in_specs=specs,
        out_specs=[VMEM_SPEC] * len(outputs),
        scratch_shapes=scratch,
        compiler_params=pltpu.CompilerParams(vmem_limit_bytes=VMEM_LIMIT),
    )(*inputs)


def swap(value, axis, mask):
    size = lax.axis_size(axis)
    return lax.ppermute(value, axis, [(i, i ^ mask) for i in range(size)])


def plus(a, b):
    return (a.astype(jnp.float32) + b.astype(jnp.float32)).astype(a.dtype)


def butterfly(value, axis, radix):
    size = lax.axis_size(axis)
    if size & (size - 1):
        return [lax.psum(value.astype(jnp.float32), axis)]
    mask, parts = 1, [value]
    while mask < size:
        terms = [p.astype(jnp.float32) for p in parts]
        while len(terms) > 1:
            terms = [terms[i] + terms[i + 1] for i in range(0, len(terms), 2)]
        total = terms[0].astype(value.dtype)
        span = min(radix, size // mask)
        parts = [total] + [swap(total, axis, mask * k) for k in range(1, span)]
        mask *= span
    return parts


def on_device(
    tiles,
    tile_row,
    tile_col,
    tile_count,
    cost,
    demand,
    upper,
    col_flag,
    row_flag,
    primal_start,
    dual_start,
):
    tile = tiles.shape[1]
    scen = primal_start.shape[0]
    col_blocks = primal_start.shape[1] // tile
    row_blocks = dual_start.shape[1] // tile
    bf16, f32 = jnp.bfloat16, jnp.float32
    cost, upper, col_flag = (v.reshape(col_blocks, tile) for v in (cost, upper, col_flag))
    row_flag = row_flag.reshape(row_blocks, tile)
    row_slot = lax.axis_index("rowblk").astype(jnp.int32).reshape(1)
    col_slot = lax.axis_index("colblk").astype(jnp.int32).reshape(1)
    grid = [tile_count, tile_row, tile_col]

    small = jax.ShapeDtypeStruct((scen, tile), f32)
    col_parts = jax.ShapeDtypeStruct((col_blocks // 2 + 1, 2 * scen, tile), bf16)
    row_parts = jax.ShapeDtypeStruct((row_blocks // 2 + 1, 2 * scen, tile), bf16)
    primal = jax.ShapeDtypeStruct(primal_start.shape, f32)
    dual_like = jax.ShapeDtypeStruct(dual_start.shape, f32)
    to_cols = [
        pltpu.VMEM((row_blocks, 2 * scen, tile), bf16),
        pltpu.VMEM((col_blocks + 1, scen, tile), f32),
    ]
    to_rows = [
        pltpu.VMEM((col_blocks, 2 * scen, tile), bf16),
        pltpu.VMEM((row_blocks + 1, scen, tile), f32),
    ]

    point, dual = primal_start, dual_start
    weight = jnp.ones((scen, tile), f32)
    primal_norm = weight
    (terms,) = call(first_kernel, [*grid, tiles, dual], [col_parts], to_cols, 3)
    for step in range(ITERS):
        mix = (step + 1.0) / (step + 2.0)
        last = step == ITERS - 1
        parts = butterfly(terms, "rowblk", 2)
        point, weight, terms = call(
            functools.partial(primal_kernel, mix, len(parts)),
            [*grid, col_slot, tiles, *parts, weight, primal_norm, cost, upper, col_flag, point, primal_start],
            [primal, small, row_parts],
            to_rows,
            4,
        )
        parts = butterfly(terms, "colblk", 4)
        dual, primal_norm, terms = call(
            functools.partial(dual_kernel, mix, last, len(parts)),
            [*grid, row_slot, tiles, *parts, weight, demand, row_flag, dual, dual_start],
            [dual_like, small, small if last else col_parts],
            [] if last else to_cols,
            4,
        )
    parts = butterfly(terms, "rowblk", 4)
    dual_norm = jnp.sum(functools.reduce(jnp.add, parts), axis=1)
    ratio = (dual_norm + EPS) / (primal_norm[:, 0] + EPS)
    weight = jnp.sqrt(weight[:, 0] * jnp.sqrt(ratio))
    return point, dual, weight


def solution(mesh):
    return jax.shard_map(
        on_device,
        mesh=mesh,
        in_specs=(
            P(("groups", "rowblk", "colblk"), None, None),
            P(("groups", "rowblk", "colblk")),
            P(("groups", "rowblk", "colblk")),
            P(("groups", "rowblk", "colblk")),
            P(("groups", "colblk")),
            P(None, ("groups", "rowblk")),
            P(("groups", "colblk")),
            P(("groups", "colblk")),
            P(("groups", "rowblk")),
            P(None, ("groups", "colblk")),
            P(None, ("groups", "rowblk")),
        ),
        out_specs=(P(None, ("groups", "colblk")), P(None, ("groups", "rowblk")), P("groups")),
        check_vma=False,
    )
```

```python
import functools

import jax
import jax.numpy as jnp
from jax import lax
from jax.experimental import pallas as pl
from jax.experimental.pallas import tpu as pltpu
from jax.sharding import PartitionSpec as P

ITERS = 2
ETA = 0.3
EPS = 1e-06
PART = 32
VMEM_LIMIT = 8 * 1024 * 1024

SMEM_SPEC = pl.BlockSpec(memory_space=pltpu.SMEM)
VMEM_SPEC = pl.BlockSpec(memory_space=pltpu.VMEM)
FAR_SPEC = pl.BlockSpec(memory_space=pltpu.HBM)


def split_rows(value):
    high = value.astype(jnp.bfloat16)
    low = (value - high.astype(jnp.float32)).astype(jnp.bfloat16)
    return jnp.concatenate([high, low], axis=0)


def fetch_grid(grid, held, sems):
    copies = [pltpu.make_async_copy(a, b, sems.at[i]) for i, (a, b) in enumerate(zip(grid[1:], held))]
    for copy in copies:
        copy.start()
    return copies


def tile_products(grid, tiles, source, acc, backward, ready=None):
    count, rows, cols = grid
    total, tile = tiles.shape[0], tiles.shape[1]
    spare = acc.shape[0] - 1
    scen = acc.shape[1]
    live = count[0]
    depth = 0 if backward else 1
    dims = (((1,), (depth,)), ((), ()))
    acc[...] = jnp.zeros_like(acc)

    def part(first, size):
        if ready is not None:
            ready(first)
        landing, results = [], []
        for g in range(first, first + size):
            goes = cols[g] if backward else rows[g]
            landing.append(jnp.where(g < live, goes, spare))
        pair = 2 if size % 2 == 0 else 1
        for g in range(first, first + size, pair):
            picked = [source[rows[g + k] if backward else cols[g + k]] for k in range(pair)]
            if pair == 2:
                blank = jnp.zeros_like(picked[0])
                left = jnp.concatenate(
                    [
                        jnp.concatenate([picked[0], blank], axis=1),
                        jnp.concatenate([blank, picked[1]], axis=1),
                    ],
                    axis=0,
                )
                right = jnp.concatenate([tiles[g], tiles[g + 1]], axis=depth)
            else:
                left, right = picked[0], tiles[g]
            product = lax.dot_general(left, right, dims, preferred_element_type=jnp.float32)
            for k in range(pair):
                own = product[2 * scen * k : 2 * scen * (k + 1)]
                results.append(own[:scen] + own[scen:])
        for where, value in zip(landing, results):
            acc[where] += value

    for first in range(0, total, PART):
        size = min(PART, total - first)
        if first == 0:
            part(first, size)
        else:
            pl.when(first < live)(functools.partial(part, first, size))


def pack(acc, out, norm, slot):
    half = (acc.shape[0] - 1) // 2
    for b in range(half):
        out[b] = jnp.concatenate([acc[b], acc[b + half]], axis=0).astype(jnp.bfloat16)
    lanes = lax.broadcasted_iota(jnp.int32, (acc.shape[1], acc.shape[2]), 1)
    out[half] = split_rows(jnp.where(lanes == slot, norm, 0.0))


def add_up(terms):
    while len(terms) > 1:
        terms = [terms[i] + terms[i + 1] for i in range(0, len(terms), 2)]
    return terms[0]


def unpack(parts, half):
    scen = parts[0].shape[1] // 2
    for k in range(half):
        both = add_up([p[k].astype(jnp.float32) for p in parts])
        yield k, both[:scen]
        yield k + half, both[scen:]


def unpack_norm(parts, half):
    both = add_up([p[half].astype(jnp.float32) for p in parts])
    scen = both.shape[0] // 2
    return jnp.sum(both[:scen] + both[scen:], axis=1, keepdims=True)


def first_kernel(*refs):
    grid, (tiles_far, dual_far), (out, tiles), (source, acc), held, (dual, sems) = (
        refs[:3], refs[3:5], refs[5:7], refs[7:9], refs[9:11], refs[11:]
    )
    tile = tiles.shape[1]
    get_dual = pltpu.make_async_copy(dual_far, dual, sems.at[2])
    get_dual.start()
    copies = fetch_grid(grid, held, sems)
    get_tiles = {}
    for n, first in enumerate(range(0, tiles.shape[0], PART)):
        span = pl.ds(first, min(PART, tiles.shape[0] - first))
        get_tiles[first] = pltpu.make_async_copy(tiles_far.at[span], tiles.at[span], sems.at[3 + n])
        get_tiles[first].start()
    get_dual.wait()
    for b in range(source.shape[0]):
        source[b] = split_rows(dual[:, b * tile : (b + 1) * tile])
    for copy in copies:
        copy.wait()
    tile_products((grid[0], *held), tiles, source, acc, True, lambda first: get_tiles[first].wait())
    for first in list(get_tiles)[1:]:
        pl.when(first >= grid[0][0])(get_tiles[first].wait)
    pack(acc, out, 0.0, 0)


def primal_kernel(mix, last, n_parts, *refs):
    grid, slot, tiles = refs[:3], refs[3], refs[4]
    parts = refs[5 : 5 + n_parts]
    refs = refs[5 + n_parts :]
    weight_in, primal_norm, cost, upper, flag, point, start = refs[:7]
    point_out, weight_out, out, source, acc, *held = refs[7:14]
    sems = refs[14]
    copies = fetch_grid(grid, held, sems)
    made = refs[15] if last else point_out
    tile = tiles.shape[1]
    blocks = source.shape[0]
    half = blocks // 2
    if mix > 0.5:
        dual_norm = unpack_norm(parts, half)
        weight = weight_in[:, :1]
        ratio = (dual_norm + EPS) / (primal_norm[:, :1] + EPS)
        weight = jnp.sqrt(weight * jnp.sqrt(ratio))
        weight_out[...] = jnp.broadcast_to(weight, weight_out.shape)
        tau = ETA / weight
    else:
        weight_out[...] = weight_in[...]
        tau = ETA / weight_in[:, :1]
    tau = jnp.broadcast_to(tau, (tau.shape[0], tile))
    moved_norm = jnp.zeros_like(tau)
    for b, value in unpack(parts, half):
        lanes = slice(b * tile, (b + 1) * tile)
        old = point[:, lanes]
        moved = old - tau * (cost[b : b + 1, :] - value)
        limit = jnp.where(flag[b : b + 1, :] > 0, upper[b : b + 1, :], jnp.inf)
        x_hat = jnp.maximum(jnp.minimum(moved, limit), 0.0)
        step = x_hat - old
        moved_norm += step * step
        x_bar = 2.0 * x_hat - old
        made[:, lanes] = mix * x_bar + (1.0 - mix) * start[:, lanes]
        source[b] = split_rows(x_bar)
    if last:
        put = pltpu.make_async_copy(made, point_out, sems.at[2])
        put.start()
    for copy in copies:
        copy.wait()
    tile_products((grid[0], *held), tiles, source, acc, False)
    pack(acc, out, jnp.sum(moved_norm, axis=1, keepdims=True), slot[0])
    if last:
        put.wait()


def dual_kernel(mix, last, n_parts, *refs):
    if last:
        slot, refs = refs[0], refs[1:]
    else:
        grid, slot, tiles, refs = refs[:3], refs[3], refs[4], refs[5:]
    parts = refs[:n_parts]
    refs = refs[n_parts:]
    weight, demand, flag, dual, start = refs[:5]
    if last:
        dual_out, primal_norm, out, made, sems = refs[5:]
    else:
        dual_out, primal_norm, out, source, acc, *held = refs[5:12]
        copies = fetch_grid(grid, held, refs[12])
        made = dual_out
    tile = flag.shape[1]
    blocks = flag.shape[0]
    half = blocks // 2
    primal_norm[...] = jnp.broadcast_to(unpack_norm(parts, half), primal_norm.shape)
    sigma = ETA * weight[...]
    moved_norm = jnp.zeros_like(sigma)
    for b, value in unpack(parts, half):
        lanes = slice(b * tile, (b + 1) * tile)
        old = dual[:, lanes]
        moved = old + sigma * (demand[:, lanes] - value)
        floor = jnp.where(flag[b : b + 1, :] > 0, 0.0, -jnp.inf)
        y_hat = jnp.maximum(moved, floor)
        step = y_hat - old
        moved_norm += step * step
        new = mix * (2.0 * y_hat - old) + (1.0 - mix) * start[:, lanes]
        made[:, lanes] = new
        if not last:
            source[b] = split_rows(new)
    if last:
        put = pltpu.make_async_copy(made, dual_out, sems.at[0])
        put.start()
    dual_norm = jnp.sum(moved_norm, axis=1, keepdims=True)
    if last:
        lanes = lax.broadcasted_iota(jnp.int32, out.shape, 1)
        out[...] = jnp.where(lanes == slot[0], dual_norm, 0.0)
        put.wait()
    else:
        for copy in copies:
            copy.wait()
        tile_products((grid[0], *held), tiles, source, acc, True)
        pack(acc, out, dual_norm, slot[0])


def call(kernel, inputs, in_specs, outputs, out_specs, scratch):
    return pl.pallas_call(
        kernel,
        out_shape=outputs,
        in_specs=in_specs,
        out_specs=out_specs,
        scratch_shapes=scratch,
        compiler_params=pltpu.CompilerParams(vmem_limit_bytes=VMEM_LIMIT),
    )(*inputs)


def far(value):
    return pltpu.with_memory_space_constraint(value, pltpu.HBM)


def swap(value, axis, mask):
    size = lax.axis_size(axis)
    return lax.ppermute(value, axis, [(i, i ^ mask) for i in range(size)])


def butterfly(value, axis, radix):
    size = lax.axis_size(axis)
    if size & (size - 1):
        return [lax.psum(value.astype(jnp.float32), axis)]
    mask, parts = 1, [value]
    while mask < size:
        total = add_up([p.astype(jnp.float32) for p in parts]).astype(value.dtype)
        span = min(radix, size // mask)
        parts = [total] + [swap(total, axis, mask * k) for k in range(1, span)]
        mask *= span
    return parts


def on_device(
    tiles,
    tile_row,
    tile_col,
    tile_count,
    cost,
    demand,
    upper,
    col_flag,
    row_flag,
    primal_start,
    dual_start,
):
    tile = tiles.shape[1]
    scen = primal_start.shape[0]
    col_blocks = primal_start.shape[1] // tile
    row_blocks = dual_start.shape[1] // tile
    bf16, f32 = jnp.bfloat16, jnp.float32
    cost, upper, col_flag = (v.reshape(col_blocks, tile) for v in (cost, upper, col_flag))
    row_flag = row_flag.reshape(row_blocks, tile)
    row_slot = lax.axis_index("rowblk").astype(jnp.int32).reshape(1)
    col_slot = lax.axis_index("colblk").astype(jnp.int32).reshape(1)
    grid = [tile_count, far(tile_row), far(tile_col)]

    total = tile_row.shape[0]
    small = jax.ShapeDtypeStruct((scen, tile), f32)
    col_parts = jax.ShapeDtypeStruct((col_blocks // 2 + 1, 2 * scen, tile), bf16)
    row_parts = jax.ShapeDtypeStruct((row_blocks // 2 + 1, 2 * scen, tile), bf16)
    primal = jax.ShapeDtypeStruct(primal_start.shape, f32)
    dual_like = jax.ShapeDtypeStruct(dual_start.shape, f32)
    held = [pltpu.SMEM((total,), jnp.int32)] * 2
    sems = pltpu.SemaphoreType.DMA((3 + pl.cdiv(total, PART),))
    to_cols = [
        pltpu.VMEM((row_blocks, 2 * scen, tile), bf16),
        pltpu.VMEM((col_blocks + 1, scen, tile), f32),
        *held,
    ]
    to_rows = [
        pltpu.VMEM((col_blocks, 2 * scen, tile), bf16),
        pltpu.VMEM((row_blocks + 1, scen, tile), f32),
        *held,
    ]

    point, dual = primal_start, dual_start
    weight = jnp.ones((scen, tile), f32)
    primal_norm = weight
    terms, tiles = call(
        first_kernel,
        [*grid, far(tiles), far(dual)],
        [SMEM_SPEC] + [FAR_SPEC] * 4,
        [col_parts, pltpu.VMEM(tiles.shape, tiles.dtype)],
        [VMEM_SPEC] * 2,
        [*to_cols, pltpu.VMEM(dual.shape, f32), sems],
    )
    for step in range(ITERS):
        mix = (step + 1.0) / (step + 2.0)
        last = step == ITERS - 1
        parts = butterfly(terms, "rowblk", 2)
        point, weight, terms = call(
            functools.partial(primal_kernel, mix, last, len(parts)),
            [*grid, col_slot, tiles, *parts, weight, primal_norm, cost, upper, col_flag, point, primal_start],
            [SMEM_SPEC] + [FAR_SPEC] * 2 + [SMEM_SPEC] + [VMEM_SPEC] * (8 + len(parts)),
            [primal, small, row_parts],
            [FAR_SPEC if last else VMEM_SPEC, VMEM_SPEC, VMEM_SPEC],
            [*to_rows, sems] + [pltpu.VMEM(primal.shape, f32)] * last,
        )
        parts = butterfly(terms, "colblk", 4)
        vectors = [*parts, weight, demand, row_flag, dual, dual_start]
        if last:
            dual, primal_norm, terms = call(
                functools.partial(dual_kernel, mix, last, len(parts)),
                [row_slot, *vectors],
                [SMEM_SPEC] + [VMEM_SPEC] * len(vectors),
                [dual_like, small, small],
                [FAR_SPEC, VMEM_SPEC, VMEM_SPEC],
                [pltpu.VMEM(dual.shape, f32), sems],
            )
        else:
            dual, primal_norm, terms = call(
                functools.partial(dual_kernel, mix, last, len(parts)),
                [*grid, row_slot, tiles, *vectors],
                [SMEM_SPEC] + [FAR_SPEC] * 2 + [SMEM_SPEC] + [VMEM_SPEC] * (1 + len(vectors)),
                [dual_like, small, col_parts],
                [VMEM_SPEC] * 3,
                [*to_cols, sems],
            )
    parts = butterfly(terms, "rowblk", 4)
    dual_norm = jnp.sum(functools.reduce(jnp.add, parts), axis=1)
    ratio = (dual_norm + EPS) / (primal_norm[:, 0] + EPS)
    weight = jnp.sqrt(weight[:, 0] * jnp.sqrt(ratio))
    return point, dual, weight


def solution(mesh):
    return jax.shard_map(
        on_device,
        mesh=mesh,
        in_specs=(
            P(("groups", "rowblk", "colblk"), None, None),
            P(("groups", "rowblk", "colblk")),
            P(("groups", "rowblk", "colblk")),
            P(("groups", "rowblk", "colblk")),
            P(("groups", "colblk")),
            P(None, ("groups", "rowblk")),
            P(("groups", "colblk")),
            P(("groups", "colblk")),
            P(("groups", "rowblk")),
            P(None, ("groups", "colblk")),
            P(None, ("groups", "rowblk")),
        ),
        out_specs=(P(None, ("groups", "colblk")), P(None, ("groups", "rowblk")), P("groups")),
        check_vma=False,
    )
```

```python
import functools

import jax
import jax.numpy as jnp
from jax import lax
from jax.experimental import pallas as pl
from jax.experimental.pallas import tpu as pltpu
from jax.sharding import PartitionSpec as P

ITERS = 2
ETA = 0.3
EPS = 1e-06
PART = 32
VMEM_LIMIT = 8 * 1024 * 1024

SMEM_SPEC = pl.BlockSpec(memory_space=pltpu.SMEM)
VMEM_SPEC = pl.BlockSpec(memory_space=pltpu.VMEM)
FAR_SPEC = pl.BlockSpec(memory_space=pltpu.HBM)


def split_rows(value):
    high = value.astype(jnp.bfloat16)
    low = (value - high.astype(jnp.float32)).astype(jnp.bfloat16)
    return jnp.concatenate([high, low], axis=0)


def fetch_grid(grid, held, sems):
    copies = [pltpu.make_async_copy(a, b, sems.at[i]) for i, (a, b) in enumerate(zip(grid[1:], held))]
    for copy in copies:
        copy.start()
    return copies


def tile_products(grid, tiles, source, acc, backward, ready=None):
    count, rows, cols = grid
    total, tile = tiles.shape[0], tiles.shape[1]
    spare = acc.shape[0] - 1
    scen = acc.shape[1]
    live = count[0]
    depth = 0 if backward else 1
    dims = (((1,), (depth,)), ((), ()))
    acc[...] = jnp.zeros_like(acc)

    def part(first, size):
        if ready is not None:
            ready(first)
        landing, results = [], []
        for g in range(first, first + size):
            goes = cols[g] if backward else rows[g]
            landing.append(jnp.where(g < live, goes, spare))
        pair = 2 if size % 2 == 0 else 1
        for g in range(first, first + size, pair):
            picked = [source[rows[g + k] if backward else cols[g + k]] for k in range(pair)]
            if pair == 2:
                blank = jnp.zeros_like(picked[0])
                left = jnp.concatenate(
                    [
                        jnp.concatenate([picked[0], blank], axis=1),
                        jnp.concatenate([blank, picked[1]], axis=1),
                    ],
                    axis=0,
                )
                right = jnp.concatenate([tiles[g], tiles[g + 1]], axis=depth)
            else:
                left, right = picked[0], tiles[g]
            product = lax.dot_general(left, right, dims, preferred_element_type=jnp.float32)
            for k in range(pair):
                own = product[2 * scen * k : 2 * scen * (k + 1)]
                results.append(own[:scen] + own[scen:])
        for where, value in zip(landing, results):
            acc[where] += value

    for first in range(0, total, PART):
        size = min(PART, total - first)
        if first == 0:
            part(first, size)
        else:
            pl.when(first < live)(functools.partial(part, first, size))


def pack(acc, out, norm, slot):
    half = (acc.shape[0] - 1) // 2
    for b in range(half):
        out[b] = jnp.concatenate([acc[b], acc[b + half]], axis=0).astype(jnp.bfloat16)
    lanes = lax.broadcasted_iota(jnp.int32, (acc.shape[1], acc.shape[2]), 1)
    out[half] = split_rows(jnp.where(lanes == slot, norm, 0.0))


def add_up(terms):
    while len(terms) > 1:
        terms = [terms[i] + terms[i + 1] for i in range(0, len(terms), 2)]
    return terms[0]


def unpack(parts, half):
    scen = parts[0].shape[1] // 2
    for k in range(half):
        both = add_up([p[k].astype(jnp.float32) for p in parts])
        yield k, both[:scen]
        yield k + half, both[scen:]


def unpack_norm(parts, half):
    both = add_up([p[half].astype(jnp.float32) for p in parts])
    scen = both.shape[0] // 2
    return jnp.sum(both[:scen] + both[scen:], axis=1, keepdims=True)


def first_kernel(*refs):
    grid, (tiles_far, dual_far), (out, tiles), (source, acc), held, (dual, sems) = (
        refs[:3], refs[3:5], refs[5:7], refs[7:9], refs[9:11], refs[11:]
    )
    tile = tiles.shape[1]
    get_dual = pltpu.make_async_copy(dual_far, dual, sems.at[2])
    get_dual.start()
    copies = fetch_grid(grid, held, sems)
    get_tiles = {}
    for n, first in enumerate(range(0, tiles.shape[0], PART)):
        span = pl.ds(first, min(PART, tiles.shape[0] - first))
        get_tiles[first] = pltpu.make_async_copy(tiles_far.at[span], tiles.at[span], sems.at[3 + n])
        get_tiles[first].start()
    get_dual.wait()
    for b in range(source.shape[0]):
        source[b] = split_rows(dual[:, b * tile : (b + 1) * tile])
    for copy in copies:
        copy.wait()
    tile_products((grid[0], *held), tiles, source, acc, True, lambda first: get_tiles[first].wait())
    for first in list(get_tiles)[1:]:
        pl.when(first >= grid[0][0])(get_tiles[first].wait)
    pack(acc, out, 0.0, 0)


def primal_kernel(mix, last, n_parts, *refs):
    grid, tiles = refs[:3], refs[3]
    parts = refs[4 : 4 + n_parts]
    refs = refs[4 + n_parts :]
    slot = lax.axis_index("colblk")
    weight_in, primal_norm, cost, upper, flag, point, start = refs[:7]
    point_out, weight_out, out, source, acc, *held = refs[7:14]
    sems = refs[14]
    copies = fetch_grid(grid, held, sems)
    made = refs[15] if last else point_out
    tile = tiles.shape[1]
    blocks = source.shape[0]
    half = blocks // 2
    if mix > 0.5:
        dual_norm = unpack_norm(parts, half)
        weight = weight_in[:, :1]
        ratio = (dual_norm + EPS) / (primal_norm[:, :1] + EPS)
        weight = jnp.sqrt(weight * jnp.sqrt(ratio))
        weight_out[...] = jnp.broadcast_to(weight, weight_out.shape)
        tau = ETA / weight
    else:
        weight_out[...] = weight_in[...]
        tau = ETA / weight_in[:, :1]
    tau = jnp.broadcast_to(tau, (tau.shape[0], tile))
    moved_norm = jnp.zeros_like(tau)
    for b, value in unpack(parts, half):
        lanes = slice(b * tile, (b + 1) * tile)
        old = point[:, lanes]
        moved = old - tau * (cost[b : b + 1, :] - value)
        limit = jnp.where(flag[b : b + 1, :] > 0, upper[b : b + 1, :], jnp.inf)
        x_hat = jnp.maximum(jnp.minimum(moved, limit), 0.0)
        step = x_hat - old
        moved_norm += step * step
        x_bar = 2.0 * x_hat - old
        made[:, lanes] = mix * x_bar + (1.0 - mix) * start[:, lanes]
        source[b] = split_rows(x_bar)
    if last:
        put = pltpu.make_async_copy(made, point_out, sems.at[2])
        put.start()
    for copy in copies:
        copy.wait()
    tile_products((grid[0], *held), tiles, source, acc, False)
    pack(acc, out, jnp.sum(moved_norm, axis=1, keepdims=True), slot)
    if last:
        put.wait()


def dual_kernel(mix, last, n_parts, *refs):
    if not last:
        grid, tiles, refs = refs[:3], refs[3], refs[4:]
    slot = lax.axis_index("rowblk")
    parts = refs[:n_parts]
    refs = refs[n_parts:]
    weight, demand, flag, dual, start = refs[:5]
    if last:
        dual_out, primal_norm, out, made, sems = refs[5:]
    else:
        dual_out, primal_norm, out, source, acc, *held = refs[5:12]
        copies = fetch_grid(grid, held, refs[12])
        made = dual_out
    tile = flag.shape[1]
    blocks = flag.shape[0]
    half = blocks // 2
    primal_norm[...] = jnp.broadcast_to(unpack_norm(parts, half), primal_norm.shape)
    sigma = ETA * weight[...]
    moved_norm = jnp.zeros_like(sigma)
    for b, value in unpack(parts, half):
        lanes = slice(b * tile, (b + 1) * tile)
        old = dual[:, lanes]
        moved = old + sigma * (demand[:, lanes] - value)
        floor = jnp.where(flag[b : b + 1, :] > 0, 0.0, -jnp.inf)
        y_hat = jnp.maximum(moved, floor)
        step = y_hat - old
        moved_norm += step * step
        new = mix * (2.0 * y_hat - old) + (1.0 - mix) * start[:, lanes]
        made[:, lanes] = new
        if not last:
            source[b] = split_rows(new)
    if last:
        put = pltpu.make_async_copy(made, dual_out, sems.at[0])
        put.start()
    dual_norm = jnp.sum(moved_norm, axis=1, keepdims=True)
    if last:
        lanes = lax.broadcasted_iota(jnp.int32, out.shape, 1)
        out[...] = jnp.where(lanes == slot, dual_norm, 0.0)
        put.wait()
    else:
        for copy in copies:
            copy.wait()
        tile_products((grid[0], *held), tiles, source, acc, True)
        pack(acc, out, dual_norm, slot)


def call(kernel, inputs, in_specs, outputs, out_specs, scratch):
    return pl.pallas_call(
        kernel,
        out_shape=outputs,
        in_specs=in_specs,
        out_specs=out_specs,
        scratch_shapes=scratch,
        compiler_params=pltpu.CompilerParams(vmem_limit_bytes=VMEM_LIMIT),
    )(*inputs)


def far(value):
    return pltpu.with_memory_space_constraint(value, pltpu.HBM)


def swap(value, axis, mask):
    size = lax.axis_size(axis)
    return lax.ppermute(value, axis, [(i, i ^ mask) for i in range(size)])


def butterfly(value, axis, radix):
    size = lax.axis_size(axis)
    if size & (size - 1):
        return [lax.psum(value.astype(jnp.float32), axis)]
    mask, parts = 1, [value]
    while mask < size:
        total = add_up([p.astype(jnp.float32) for p in parts]).astype(value.dtype)
        span = min(radix, size // mask)
        parts = [total] + [swap(total, axis, mask * k) for k in range(1, span)]
        mask *= span
    return parts


def on_device(
    tiles,
    tile_row,
    tile_col,
    tile_count,
    cost,
    demand,
    upper,
    col_flag,
    row_flag,
    primal_start,
    dual_start,
):
    tile = tiles.shape[1]
    scen = primal_start.shape[0]
    col_blocks = primal_start.shape[1] // tile
    row_blocks = dual_start.shape[1] // tile
    bf16, f32 = jnp.bfloat16, jnp.float32
    cost, upper, col_flag = (v.reshape(col_blocks, tile) for v in (cost, upper, col_flag))
    row_flag = row_flag.reshape(row_blocks, tile)
    grid = [tile_count, far(tile_row), far(tile_col)]

    total = tile_row.shape[0]
    small = jax.ShapeDtypeStruct((scen, tile), f32)
    col_parts = jax.ShapeDtypeStruct((col_blocks // 2 + 1, 2 * scen, tile), bf16)
    row_parts = jax.ShapeDtypeStruct((row_blocks // 2 + 1, 2 * scen, tile), bf16)
    primal = jax.ShapeDtypeStruct(primal_start.shape, f32)
    dual_like = jax.ShapeDtypeStruct(dual_start.shape, f32)
    held = [pltpu.SMEM((total,), jnp.int32)] * 2
    sems = pltpu.SemaphoreType.DMA((3 + pl.cdiv(total, PART),))
    to_cols = [
        pltpu.VMEM((row_blocks, 2 * scen, tile), bf16),
        pltpu.VMEM((col_blocks + 1, scen, tile), f32),
        *held,
    ]
    to_rows = [
        pltpu.VMEM((col_blocks, 2 * scen, tile), bf16),
        pltpu.VMEM((row_blocks + 1, scen, tile), f32),
        *held,
    ]

    point, dual = primal_start, dual_start
    weight = jnp.ones((scen, tile), f32)
    primal_norm = weight
    terms, tiles = call(
        first_kernel,
        [*grid, far(tiles), far(dual)],
        [SMEM_SPEC] + [FAR_SPEC] * 4,
        [col_parts, pltpu.VMEM(tiles.shape, tiles.dtype)],
        [VMEM_SPEC] * 2,
        [*to_cols, pltpu.VMEM(dual.shape, f32), sems],
    )
    for step in range(ITERS):
        mix = (step + 1.0) / (step + 2.0)
        last = step == ITERS - 1
        parts = butterfly(terms, "rowblk", 2)
        point, weight, terms = call(
            functools.partial(primal_kernel, mix, last, len(parts)),
            [*grid, tiles, *parts, weight, primal_norm, cost, upper, col_flag, point, primal_start],
            [SMEM_SPEC] + [FAR_SPEC] * 2 + [VMEM_SPEC] * (8 + len(parts)),
            [primal, small, row_parts],
            [FAR_SPEC if last else VMEM_SPEC, VMEM_SPEC, VMEM_SPEC],
            [*to_rows, sems] + [pltpu.VMEM(primal.shape, f32)] * last,
        )
        parts = butterfly(terms, "colblk", 4)
        vectors = [*parts, weight, demand, row_flag, dual, dual_start]
        if last:
            dual, primal_norm, terms = call(
                functools.partial(dual_kernel, mix, last, len(parts)),
                vectors,
                [VMEM_SPEC] * len(vectors),
                [dual_like, small, small],
                [FAR_SPEC, VMEM_SPEC, VMEM_SPEC],
                [pltpu.VMEM(dual.shape, f32), sems],
            )
        else:
            dual, primal_norm, terms = call(
                functools.partial(dual_kernel, mix, last, len(parts)),
                [*grid, tiles, *vectors],
                [SMEM_SPEC] + [FAR_SPEC] * 2 + [VMEM_SPEC] * (1 + len(vectors)),
                [dual_like, small, col_parts],
                [VMEM_SPEC] * 3,
                [*to_cols, sems],
            )
    parts = butterfly(terms, "rowblk", 4)
    dual_norm = jnp.sum(functools.reduce(jnp.add, parts), axis=1)
    ratio = (dual_norm + EPS) / (primal_norm[:, 0] + EPS)
    weight = jnp.sqrt(weight[:, 0] * jnp.sqrt(ratio))
    return point, dual, weight


def solution(mesh):
    return jax.shard_map(
        on_device,
        mesh=mesh,
        in_specs=(
            P(("groups", "rowblk", "colblk"), None, None),
            P(("groups", "rowblk", "colblk")),
            P(("groups", "rowblk", "colblk")),
            P(("groups", "rowblk", "colblk")),
            P(("groups", "colblk")),
            P(None, ("groups", "rowblk")),
            P(("groups", "colblk")),
            P(("groups", "colblk")),
            P(("groups", "rowblk")),
            P(None, ("groups", "colblk")),
            P(None, ("groups", "rowblk")),
        ),
        out_specs=(P(None, ("groups", "colblk")), P(None, ("groups", "rowblk")), P("groups")),
        check_vma=False,
    )
```

```python
import functools

import jax
import jax.numpy as jnp
from jax import lax
from jax.experimental import pallas as pl
from jax.experimental.pallas import tpu as pltpu
from jax.sharding import PartitionSpec as P

ITERS = 2
ETA = 0.3
EPS = 1e-06
PART = 24
VMEM_LIMIT = 8 * 1024 * 1024

SMEM_SPEC = pl.BlockSpec(memory_space=pltpu.SMEM)
VMEM_SPEC = pl.BlockSpec(memory_space=pltpu.VMEM)
FAR_SPEC = pl.BlockSpec(memory_space=pltpu.HBM)


def split_rows(value):
    high = value.astype(jnp.bfloat16)
    low = (value - high.astype(jnp.float32)).astype(jnp.bfloat16)
    return jnp.concatenate([high, low], axis=0)


def tile_products(grid, tiles, source, acc, backward, ready=None):
    count, rows, cols = grid
    total, tile = tiles.shape[0], tiles.shape[1]
    spare = acc.shape[0] - 1
    scen = acc.shape[1]
    live = count[0]
    acc[...] = jnp.zeros_like(acc)

    def part(first, size):
        if ready is not None:
            ready(first)
        landing, results = [], []
        for g in range(first, first + size):
            goes = cols[g] if backward else rows[g]
            landing.append(jnp.where(g < live, goes, spare))
        pair = 2 if size % 2 == 0 else 1
        for g in range(first, first + size, pair):
            picked = [source[rows[g + k] if backward else cols[g + k]] for k in range(pair)]
            if pair == 2:
                blank = jnp.zeros_like(picked[0])
                left = jnp.concatenate(
                    [
                        jnp.concatenate([picked[0], blank], axis=1),
                        jnp.concatenate([blank, picked[1]], axis=1),
                    ],
                    axis=0,
                )
                right = jnp.concatenate([tiles[g], tiles[g + 1]], axis=0)
            else:
                left, right = picked[0], tiles[g]
            product = jnp.dot(left, right, preferred_element_type=jnp.float32)
            for k in range(pair):
                own = product[2 * scen * k : 2 * scen * (k + 1)]
                results.append(own[:scen] + own[scen:])
        for where, value in zip(landing, results):
            acc[where] += value

    for first in range(0, total, PART):
        size = min(PART, total - first)
        if first == 0:
            part(first, size)
        else:
            pl.when(first < live)(functools.partial(part, first, size))


def pack(acc, out, norm, slot):
    half = (acc.shape[0] - 1) // 2
    for b in range(half):
        out[b] = jnp.concatenate([acc[b], acc[b + half]], axis=0).astype(jnp.bfloat16)
    lanes = lax.broadcasted_iota(jnp.int32, (acc.shape[1], acc.shape[2]), 1)
    out[half] = split_rows(jnp.where(lanes == slot, norm, 0.0))


def add_up(terms):
    while len(terms) > 1:
        terms = [terms[i] + terms[i + 1] for i in range(0, len(terms), 2)]
    return terms[0]


def unpack(parts, half):
    scen = parts[0].shape[1] // 2
    for k in range(half):
        both = add_up([p[k].astype(jnp.float32) for p in parts])
        yield k, both[:scen]
        yield k + half, both[scen:]


def unpack_norm(parts, half):
    both = add_up([p[half].astype(jnp.float32) for p in parts])
    scen = both.shape[0] // 2
    return jnp.sum(both[:scen] + both[scen:], axis=1, keepdims=True)


def first_kernel(*refs):
    count, rows_far, cols_far, tiles_far, dual_far, out, tiles, rows, cols, source, acc, dual, sems = refs
    tile = tiles.shape[1]
    get_dual = pltpu.make_async_copy(dual_far, dual, sems.at[2])
    get_dual.start()
    copies = [
        pltpu.make_async_copy(rows_far, rows, sems.at[0]),
        pltpu.make_async_copy(cols_far, cols, sems.at[1]),
    ]
    for copy in copies:
        copy.start()
    get_tiles = {}
    for n, first in enumerate(range(0, tiles.shape[0], PART)):
        span = pl.ds(first, min(PART, tiles.shape[0] - first))
        get_tiles[first] = pltpu.make_async_copy(tiles_far.at[span], tiles.at[span], sems.at[3 + n])
        get_tiles[first].start()
    get_dual.wait()
    for b in range(source.shape[0]):
        source[b] = split_rows(dual[:, b * tile : (b + 1) * tile])
    for copy in copies:
        copy.wait()
    tile_products((count, rows, cols), tiles, source, acc, True, lambda first: get_tiles[first].wait())
    for first in list(get_tiles)[1:]:
        pl.when(first >= count[0])(get_tiles[first].wait)
    pack(acc, out, 0.0, 0)


def turn_kernel(count, tiles, after, turned):
    del after
    total = tiles.shape[0]

    def part(first):
        for g in range(first, min(first + PART, total)):
            turned[g] = tiles[g].T

    for first in range(0, total, PART):
        pl.when(first < count[0])(functools.partial(part, first))


def primal_kernel(mix, last, n_parts, *refs):
    grid, tiles = refs[:3], refs[3]
    parts = refs[4 : 4 + n_parts]
    refs = refs[4 + n_parts :]
    slot = lax.axis_index("colblk")
    weight_in, primal_norm, cost, upper, flag, point, start = refs[:7]
    point_out, weight_out, out, source, acc, sems = refs[7:13]
    made = point_out
    tile = tiles.shape[1]
    blocks = source.shape[0]
    half = blocks // 2
    if mix > 0.5:
        dual_norm = unpack_norm(parts, half)
        weight = weight_in[:, :1]
        ratio = (dual_norm + EPS) / (primal_norm[:, :1] + EPS)
        weight = jnp.sqrt(weight * jnp.sqrt(ratio))
        weight_out[...] = jnp.broadcast_to(weight, weight_out.shape)
        tau = ETA / weight
    else:
        weight_out[...] = weight_in[...]
        tau = ETA / weight_in[:, :1]
    tau = jnp.broadcast_to(tau, (tau.shape[0], tile))
    moved_norm = jnp.zeros_like(tau)
    for b, value in unpack(parts, half):
        lanes = slice(b * tile, (b + 1) * tile)
        old = point[:, lanes]
        moved = old - tau * (cost[b : b + 1, :] - value)
        limit = jnp.where(flag[b : b + 1, :] > 0, upper[b : b + 1, :], jnp.inf)
        x_hat = jnp.maximum(jnp.minimum(moved, limit), 0.0)
        step = x_hat - old
        moved_norm += step * step
        x_bar = 2.0 * x_hat - old
        made[:, lanes] = mix * x_bar + (1.0 - mix) * start[:, lanes]
        source[b] = split_rows(x_bar)
    tile_products(grid, tiles, source, acc, False)
    pack(acc, out, jnp.sum(moved_norm, axis=1, keepdims=True), slot)


def dual_kernel(mix, last, n_parts, *refs):
    if not last:
        grid, tiles, refs = refs[:3], refs[3], refs[4:]
    slot = lax.axis_index("rowblk")
    parts = refs[:n_parts]
    refs = refs[n_parts:]
    weight, demand, flag, dual, start = refs[:5]
    if last:
        dual_out, primal_norm, out = refs[5:]
        made = dual_out
    else:
        dual_out, primal_norm, out, source, acc, sems = refs[5:]
        made = dual_out
    tile = flag.shape[1]
    blocks = flag.shape[0]
    half = blocks // 2
    primal_norm[...] = jnp.broadcast_to(unpack_norm(parts, half), primal_norm.shape)
    sigma = ETA * weight[...]
    moved_norm = jnp.zeros_like(sigma)
    for b, value in unpack(parts, half):
        lanes = slice(b * tile, (b + 1) * tile)
        old = dual[:, lanes]
        moved = old + sigma * (demand[:, lanes] - value)
        floor = jnp.where(flag[b : b + 1, :] > 0, 0.0, -jnp.inf)
        y_hat = jnp.maximum(moved, floor)
        step = y_hat - old
        moved_norm += step * step
        new = mix * (2.0 * y_hat - old) + (1.0 - mix) * start[:, lanes]
        made[:, lanes] = new
        if not last:
            source[b] = split_rows(new)
    dual_norm = jnp.sum(moved_norm, axis=1, keepdims=True)
    if last:
        lanes = lax.broadcasted_iota(jnp.int32, out.shape, 1)
        out[...] = jnp.where(lanes == slot, dual_norm, 0.0)
    else:
        tile_products(grid, tiles, source, acc, True)
        pack(acc, out, dual_norm, slot)


def call(kernel, inputs, in_specs, outputs, out_specs, scratch, cost=None):
    return pl.pallas_call(
        kernel,
        out_shape=outputs,
        in_specs=in_specs,
        out_specs=out_specs,
        scratch_shapes=scratch,
        cost_estimate=cost,
        compiler_params=pltpu.CompilerParams(vmem_limit_bytes=VMEM_LIMIT),
    )(*inputs)


def far(value):
    return pltpu.with_memory_space_constraint(value, pltpu.HBM)


def swap(value, axis, mask):
    size = lax.axis_size(axis)
    return lax.ppermute(value, axis, [(i, i ^ mask) for i in range(size)])


def butterfly(value, axis, radix):
    size = lax.axis_size(axis)
    if size & (size - 1):
        return [lax.psum(value.astype(jnp.float32), axis)]
    mask, parts = 1, [value]
    while mask < size:
        total = add_up([p.astype(jnp.float32) for p in parts]).astype(value.dtype)
        span = min(radix, size // mask)
        parts = [total] + [swap(total, axis, mask * k) for k in range(1, span)]
        mask *= span
    return parts


def on_device(
    tiles,
    tile_row,
    tile_col,
    tile_count,
    cost,
    demand,
    upper,
    col_flag,
    row_flag,
    primal_start,
    dual_start,
):
    tile = tiles.shape[1]
    scen = primal_start.shape[0]
    col_blocks = primal_start.shape[1] // tile
    row_blocks = dual_start.shape[1] // tile
    bf16, f32 = jnp.bfloat16, jnp.float32
    cost, upper, col_flag = (v.reshape(col_blocks, tile) for v in (cost, upper, col_flag))
    row_flag = row_flag.reshape(row_blocks, tile)
    grid = [tile_count, far(tile_row), far(tile_col)]

    total = tile_row.shape[0]
    small = jax.ShapeDtypeStruct((scen, tile), f32)
    col_parts = jax.ShapeDtypeStruct((col_blocks // 2 + 1, 2 * scen, tile), bf16)
    row_parts = jax.ShapeDtypeStruct((row_blocks // 2 + 1, 2 * scen, tile), bf16)
    primal = jax.ShapeDtypeStruct(primal_start.shape, f32)
    dual_like = jax.ShapeDtypeStruct(dual_start.shape, f32)
    sems = pltpu.SemaphoreType.DMA((3 + pl.cdiv(total, PART),))
    to_cols = [
        pltpu.VMEM((row_blocks, 2 * scen, tile), bf16),
        pltpu.VMEM((col_blocks + 1, scen, tile), f32),
    ]
    to_rows = [
        pltpu.VMEM((col_blocks, 2 * scen, tile), bf16),
        pltpu.VMEM((row_blocks + 1, scen, tile), f32),
    ]

    point, dual = primal_start, dual_start
    weight = jnp.ones((scen, tile), f32)
    primal_norm = weight
    terms, tiles, *slots = call(
        first_kernel,
        [*grid, far(tiles), far(dual)],
        [SMEM_SPEC] + [FAR_SPEC] * 4,
        [col_parts, pltpu.VMEM(tiles.shape, tiles.dtype), *[pltpu.SMEM((total,), jnp.int32)] * 2],
        [VMEM_SPEC] * 2 + [SMEM_SPEC] * 2,
        [*to_cols, pltpu.VMEM(dual.shape, f32), sems],
    )
    grid = [tile_count, *slots]
    for step in range(ITERS):
        mix = (step + 1.0) / (step + 2.0)
        last = step == ITERS - 1
        parts = butterfly(terms, "rowblk", 2)
        if step == 0:
            (turned,) = call(
                turn_kernel,
                [tile_count, tiles, parts[0]],
                [SMEM_SPEC] + [VMEM_SPEC] * 2,
                [pltpu.VMEM(tiles.shape, tiles.dtype)],
                [VMEM_SPEC],
                [],
                pl.CostEstimate(flops=0, bytes_accessed=2 * tiles.size * 2, transcendentals=0),
            )
        point, weight, terms = call(
            functools.partial(primal_kernel, mix, last, len(parts)),
            [*grid, turned, *parts, weight, primal_norm, cost, upper, col_flag, point, primal_start],
            [SMEM_SPEC] * 3 + [VMEM_SPEC] * (8 + len(parts)),
            [pltpu.VMEM(primal.shape, f32), small, row_parts],
            [VMEM_SPEC, VMEM_SPEC, VMEM_SPEC],
            [*to_rows, sems],
        )
        parts = butterfly(terms, "colblk", 4)
        vectors = [*parts, weight, demand, row_flag, dual, dual_start]
        if last:
            dual, primal_norm, terms = call(
                functools.partial(dual_kernel, mix, last, len(parts)),
                vectors,
                [VMEM_SPEC] * len(vectors),
                [pltpu.VMEM(dual.shape, f32), small, small],
                [VMEM_SPEC] * 3,
                [],
            )
        else:
            dual, primal_norm, terms = call(
                functools.partial(dual_kernel, mix, last, len(parts)),
                [*grid, tiles, *vectors],
                [SMEM_SPEC] * 3 + [VMEM_SPEC] * (1 + len(vectors)),
                [dual_like, small, col_parts],
                [VMEM_SPEC] * 3,
                [*to_cols, sems],
            )
    parts = butterfly(terms, "rowblk", 4)
    dual_norm = jnp.sum(functools.reduce(jnp.add, parts), axis=1)
    ratio = (dual_norm + EPS) / (primal_norm[:, 0] + EPS)
    weight = jnp.sqrt(weight[:, 0] * jnp.sqrt(ratio))
    return point, dual, weight


def solution(mesh):
    return jax.shard_map(
        on_device,
        mesh=mesh,
        in_specs=(
            P(("groups", "rowblk", "colblk"), None, None),
            P(("groups", "rowblk", "colblk")),
            P(("groups", "rowblk", "colblk")),
            P(("groups", "rowblk", "colblk")),
            P(("groups", "colblk")),
            P(None, ("groups", "rowblk")),
            P(("groups", "colblk")),
            P(("groups", "colblk")),
            P(("groups", "rowblk")),
            P(None, ("groups", "colblk")),
            P(None, ("groups", "rowblk")),
        ),
        out_specs=(P(None, ("groups", "colblk")), P(None, ("groups", "rowblk")), P("groups")),
        check_vma=False,
    )
```

```python
import functools

import jax
import jax.numpy as jnp
from jax import lax
from jax.experimental import pallas as pl
from jax.experimental.pallas import tpu as pltpu
from jax.sharding import PartitionSpec as P

ITERS = 2
ETA = 0.3
EPS = 1e-06
PART = 24
VMEM_LIMIT = 8 * 1024 * 1024

SMEM_SPEC = pl.BlockSpec(memory_space=pltpu.SMEM)
VMEM_SPEC = pl.BlockSpec(memory_space=pltpu.VMEM)
FAR_SPEC = pl.BlockSpec(memory_space=pltpu.HBM)


def split_rows(value):
    high = value.astype(jnp.bfloat16)
    low = (value - high.astype(jnp.float32)).astype(jnp.bfloat16)
    return jnp.concatenate([high, low], axis=0)


def tile_products(grid, tiles, source, acc, backward, ready=None):
    count, rows, cols = grid
    total, tile = tiles.shape[0], tiles.shape[1]
    spare = acc.shape[0] - 1
    scen = acc.shape[1]
    live = count[0]
    acc[...] = jnp.zeros_like(acc)

    def part(first, size):
        if ready is not None:
            ready(first)
        landing, results = [], []
        for g in range(first, first + size):
            goes = cols[g] if backward else rows[g]
            landing.append(jnp.where(g < live, goes, spare))
        pair = 2 if size % 2 == 0 else 1
        for g in range(first, first + size, pair):
            picked = [source[rows[g + k] if backward else cols[g + k]] for k in range(pair)]
            if pair == 2:
                blank = jnp.zeros_like(picked[0])
                left = jnp.concatenate(
                    [
                        jnp.concatenate([picked[0], blank], axis=1),
                        jnp.concatenate([blank, picked[1]], axis=1),
                    ],
                    axis=0,
                )
                right = jnp.concatenate([tiles[g], tiles[g + 1]], axis=0)
            else:
                left, right = picked[0], tiles[g]
            product = jnp.dot(left, right, preferred_element_type=jnp.float32)
            for k in range(pair):
                own = product[2 * scen * k : 2 * scen * (k + 1)]
                results.append(own[:scen] + own[scen:])
        for where, value in zip(landing, results):
            acc[where] += value

    for first in range(0, total, PART):
        size = min(PART, total - first)
        pl.when(first < live)(functools.partial(part, first, size))


def pack(acc, out, norm, slot):
    half = (acc.shape[0] - 1) // 2
    for b in range(half):
        out[b] = jnp.concatenate([acc[b], acc[b + half]], axis=0).astype(jnp.bfloat16)
    lanes = lax.broadcasted_iota(jnp.int32, (acc.shape[1], acc.shape[2]), 1)
    out[half] = split_rows(jnp.where(lanes == slot, norm, 0.0))


def add_up(terms):
    while len(terms) > 1:
        terms = [terms[i] + terms[i + 1] for i in range(0, len(terms), 2)]
    return terms[0]


def unpack(parts, half):
    scen = parts[0].shape[1] // 2
    for k in range(half):
        both = add_up([p[k].astype(jnp.float32) for p in parts])
        yield k, both[:scen]
        yield k + half, both[scen:]


def unpack_norm(parts, half):
    both = add_up([p[half].astype(jnp.float32) for p in parts])
    scen = both.shape[0] // 2
    return jnp.sum(both[:scen] + both[scen:], axis=1, keepdims=True)


def first_kernel(*refs):
    count, rows_far, cols_far, tiles_far, dual_far, out, tiles, rows, cols, source, acc, dual, sems = refs
    tile = tiles.shape[1]
    get_dual = pltpu.make_async_copy(dual_far, dual, sems.at[2])
    get_dual.start()
    copies = [
        pltpu.make_async_copy(rows_far, rows, sems.at[0]),
        pltpu.make_async_copy(cols_far, cols, sems.at[1]),
    ]
    for copy in copies:
        copy.start()
    get_tiles = {}
    for n, first in enumerate(range(0, tiles.shape[0], PART)):
        span = pl.ds(first, min(PART, tiles.shape[0] - first))
        get_tiles[first] = pltpu.make_async_copy(tiles_far.at[span], tiles.at[span], sems.at[3 + n])
        pl.when(first < count[0])(get_tiles[first].start)
    get_dual.wait()
    for b in range(source.shape[0]):
        source[b] = split_rows(dual[:, b * tile : (b + 1) * tile])
    for copy in copies:
        copy.wait()
    tile_products((count, rows, cols), tiles, source, acc, True, lambda first: get_tiles[first].wait())
    pack(acc, out, 0.0, 0)


def turn_kernel(count, tiles, after, turned):
    del after
    total = tiles.shape[0]

    def part(first):
        for g in range(first, min(first + PART, total)):
            turned[g] = tiles[g].T

    for first in range(0, total, PART):
        pl.when(first < count[0])(functools.partial(part, first))


def primal_kernel(mix, last, n_parts, *refs):
    grid, tiles = refs[:3], refs[3]
    parts = refs[4 : 4 + n_parts]
    refs = refs[4 + n_parts :]
    slot = lax.axis_index("colblk")
    weight_in, primal_norm, cost, upper, flag, point, start = refs[:7]
    point_out, weight_out, out, source, acc, sems = refs[7:13]
    made = point_out
    tile = tiles.shape[1]
    blocks = source.shape[0]
    half = blocks // 2
    if mix > 0.5:
        dual_norm = unpack_norm(parts, half)
        weight = weight_in[:, :1]
        ratio = (dual_norm + EPS) / (primal_norm[:, :1] + EPS)
        weight = jnp.sqrt(weight * jnp.sqrt(ratio))
        weight_out[...] = jnp.broadcast_to(weight, weight_out.shape)
        tau = ETA / weight
    else:
        weight_out[...] = weight_in[...]
        tau = ETA / weight_in[:, :1]
    tau = jnp.broadcast_to(tau, (tau.shape[0], tile))
    moved_norm = jnp.zeros_like(tau)
    for b, value in unpack(parts, half):
        lanes = slice(b * tile, (b + 1) * tile)
        old = point[:, lanes]
        moved = old - tau * (cost[b : b + 1, :] - value)
        limit = jnp.where(flag[b : b + 1, :] > 0, upper[b : b + 1, :], jnp.inf)
        x_hat = jnp.maximum(jnp.minimum(moved, limit), 0.0)
        step = x_hat - old
        moved_norm += step * step
        x_bar = 2.0 * x_hat - old
        made[:, lanes] = mix * x_bar + (1.0 - mix) * start[:, lanes]
        source[b] = split_rows(x_bar)
    tile_products(grid, tiles, source, acc, False)
    pack(acc, out, jnp.sum(moved_norm, axis=1, keepdims=True), slot)


def dual_kernel(mix, last, n_parts, *refs):
    if not last:
        grid, tiles, refs = refs[:3], refs[3], refs[4:]
    slot = lax.axis_index("rowblk")
    parts = refs[:n_parts]
    parts = [parts[0], parts[2], parts[1], parts[3]]
    refs = refs[n_parts:]
    weight, demand, flag, dual, start = refs[:5]
    if last:
        dual_out, primal_norm, out = refs[5:]
        made = dual_out
    else:
        dual_out, primal_norm, out, source, acc, sems = refs[5:]
        made = dual_out
    tile = flag.shape[1]
    blocks = flag.shape[0]
    half = blocks // 2
    primal_norm[...] = jnp.broadcast_to(unpack_norm(parts, half), primal_norm.shape)
    sigma = ETA * weight[...]
    moved_norm = jnp.zeros_like(sigma)
    for b, value in unpack(parts, half):
        lanes = slice(b * tile, (b + 1) * tile)
        old = dual[:, lanes]
        moved = old + sigma * (demand[:, lanes] - value)
        floor = jnp.where(flag[b : b + 1, :] > 0, 0.0, -jnp.inf)
        y_hat = jnp.maximum(moved, floor)
        step = y_hat - old
        moved_norm += step * step
        new = mix * (2.0 * y_hat - old) + (1.0 - mix) * start[:, lanes]
        made[:, lanes] = new
        if not last:
            source[b] = split_rows(new)
    dual_norm = jnp.sum(moved_norm, axis=1, keepdims=True)
    if last:
        lanes = lax.broadcasted_iota(jnp.int32, out.shape, 1)
        out[...] = jnp.where(lanes == slot, dual_norm, 0.0)
    else:
        tile_products(grid, tiles, source, acc, True)
        pack(acc, out, dual_norm, slot)


def call(kernel, inputs, in_specs, outputs, out_specs, scratch, cost=None):
    return pl.pallas_call(
        kernel,
        out_shape=outputs,
        in_specs=in_specs,
        out_specs=out_specs,
        scratch_shapes=scratch,
        cost_estimate=cost,
        compiler_params=pltpu.CompilerParams(vmem_limit_bytes=VMEM_LIMIT),
    )(*inputs)


def far(value):
    return pltpu.with_memory_space_constraint(value, pltpu.HBM)


def swap(value, axis, mask):
    size = lax.axis_size(axis)
    return lax.ppermute(value, axis, [(i, i ^ mask) for i in range(size)])


def butterfly(value, axis, radix):
    size = lax.axis_size(axis)
    if size & (size - 1):
        return [lax.psum(value.astype(jnp.float32), axis)]
    mask, parts = 1, [value]
    while mask < size:
        total = add_up([p.astype(jnp.float32) for p in parts]).astype(value.dtype)
        span = min(radix, size // mask)
        parts = [total] + [swap(total, axis, mask * k) for k in range(1, span)]
        mask *= span
    return parts


def on_device(
    tiles,
    tile_row,
    tile_col,
    tile_count,
    cost,
    demand,
    upper,
    col_flag,
    row_flag,
    primal_start,
    dual_start,
):
    tile = tiles.shape[1]
    scen = primal_start.shape[0]
    col_blocks = primal_start.shape[1] // tile
    row_blocks = dual_start.shape[1] // tile
    bf16, f32 = jnp.bfloat16, jnp.float32
    cost, upper, col_flag = (v.reshape(col_blocks, tile) for v in (cost, upper, col_flag))
    row_flag = row_flag.reshape(row_blocks, tile)
    grid = [tile_count, far(tile_row), far(tile_col)]

    total = tile_row.shape[0]
    small = jax.ShapeDtypeStruct((scen, tile), f32)
    col_parts = jax.ShapeDtypeStruct((col_blocks // 2 + 1, 2 * scen, tile), bf16)
    row_parts = jax.ShapeDtypeStruct((row_blocks // 2 + 1, 2 * scen, tile), bf16)
    primal = jax.ShapeDtypeStruct(primal_start.shape, f32)
    dual_like = jax.ShapeDtypeStruct(dual_start.shape, f32)
    sems = pltpu.SemaphoreType.DMA((3 + pl.cdiv(total, PART),))
    to_cols = [
        pltpu.VMEM((row_blocks, 2 * scen, tile), bf16),
        pltpu.VMEM((col_blocks + 1, scen, tile), f32),
    ]
    to_rows = [
        pltpu.VMEM((col_blocks, 2 * scen, tile), bf16),
        pltpu.VMEM((row_blocks + 1, scen, tile), f32),
    ]

    point, dual = primal_start, dual_start
    weight = jnp.ones((scen, tile), f32)
    primal_norm = weight
    terms, tiles, *slots = call(
        first_kernel,
        [*grid, far(tiles), far(dual)],
        [SMEM_SPEC] + [FAR_SPEC] * 4,
        [col_parts, pltpu.VMEM(tiles.shape, tiles.dtype), *[pltpu.SMEM((total,), jnp.int32)] * 2],
        [VMEM_SPEC] * 2 + [SMEM_SPEC] * 2,
        [*to_cols, pltpu.VMEM(dual.shape, f32), sems],
    )
    grid = [tile_count, *slots]
    for step in range(ITERS):
        mix = (step + 1.0) / (step + 2.0)
        last = step == ITERS - 1
        parts = butterfly(terms, "rowblk", 2)
        if step == 0:
            (turned,) = call(
                turn_kernel,
                [tile_count, tiles, parts[0]],
                [SMEM_SPEC] + [VMEM_SPEC] * 2,
                [pltpu.VMEM(tiles.shape, tiles.dtype)],
                [VMEM_SPEC],
                [],
                pl.CostEstimate(flops=0, bytes_accessed=2 * tiles.size * 2, transcendentals=0),
            )
        point, weight, terms = call(
            functools.partial(primal_kernel, mix, last, len(parts)),
            [*grid, turned, *parts, weight, primal_norm, cost, upper, col_flag, point, primal_start],
            [SMEM_SPEC] * 3 + [VMEM_SPEC] * (8 + len(parts)),
            [pltpu.VMEM(primal.shape, f32), small, row_parts],
            [VMEM_SPEC, VMEM_SPEC, VMEM_SPEC],
            [*to_rows, sems],
        )
        parts = butterfly(terms, "colblk", 4)
        parts = [parts[0]] + [parts[m] for m in (2, 1, 3)]
        vectors = [*parts, weight, demand, row_flag, dual, dual_start]
        if last:
            dual, primal_norm, terms = call(
                functools.partial(dual_kernel, mix, last, len(parts)),
                vectors,
                [VMEM_SPEC] * len(vectors),
                [pltpu.VMEM(dual.shape, f32), small, small],
                [VMEM_SPEC] * 3,
                [],
            )
        else:
            dual, primal_norm, terms = call(
                functools.partial(dual_kernel, mix, last, len(parts)),
                [*grid, tiles, *vectors],
                [SMEM_SPEC] * 3 + [VMEM_SPEC] * (1 + len(vectors)),
                [dual_like, small, col_parts],
                [VMEM_SPEC] * 3,
                [*to_cols, sems],
            )
    parts = butterfly(terms, "rowblk", 4)
    dual_norm = jnp.sum(functools.reduce(jnp.add, parts), axis=1)
    ratio = (dual_norm + EPS) / (primal_norm[:, 0] + EPS)
    weight = jnp.sqrt(weight[:, 0] * jnp.sqrt(ratio))
    return point, dual, weight


def solution(mesh):
    return jax.shard_map(
        on_device,
        mesh=mesh,
        in_specs=(
            P(("groups", "rowblk", "colblk"), None, None),
            P(("groups", "rowblk", "colblk")),
            P(("groups", "rowblk", "colblk")),
            P(("groups", "rowblk", "colblk")),
            P(("groups", "colblk")),
            P(None, ("groups", "rowblk")),
            P(("groups", "colblk")),
            P(("groups", "colblk")),
            P(("groups", "rowblk")),
            P(None, ("groups", "colblk")),
            P(None, ("groups", "rowblk")),
        ),
        out_specs=(P(None, ("groups", "colblk")), P(None, ("groups", "rowblk")), P("groups")),
        check_vma=False,
    )
```

```python
import functools

import jax
import jax.numpy as jnp
from jax import lax
from jax.experimental import pallas as pl
from jax.experimental.pallas import tpu as pltpu
from jax.sharding import PartitionSpec as P

ITERS = 2
ETA = 0.3
EPS = 1e-06
PART = 24
HALF_PARTS = (32, 16, 24)
VMEM_LIMIT = 8 * 1024 * 1024

SMEM_SPEC = pl.BlockSpec(memory_space=pltpu.SMEM)
VMEM_SPEC = pl.BlockSpec(memory_space=pltpu.VMEM)
FAR_SPEC = pl.BlockSpec(memory_space=pltpu.HBM)


def top(shape):
    return lax.broadcasted_iota(jnp.int32, shape, 0) < shape[0] // 2


def turn_rows(value):
    return pltpu.roll(value, value.shape[0] // 2, 0)


def upper_half(a, b):
    return jnp.where(top(a.shape), a, turn_rows(b))


def lower_half(a, b):
    return jnp.where(top(a.shape), turn_rows(a), b)


def mine_first(value, odd):
    return jnp.where(odd, turn_rows(value), value)


def split_rows(value):
    high = value.astype(jnp.bfloat16)
    low = (value - high.astype(jnp.float32)).astype(jnp.bfloat16)
    return jnp.concatenate([high, low], axis=0)


def add_up(terms):
    while len(terms) > 1:
        terms = [terms[i] + terms[i + 1] for i in range(0, len(terms), 2)]
    return terms[0]


def over_parts(tiles, live, part, sizes=(PART,)):
    total, first, n = tiles.shape[0], 0, 0
    while first < total:
        size = min(sizes[min(n, len(sizes) - 1)], total - first)
        pl.when(first < live)(functools.partial(part, first, size))
        first, n = first + size, n + 1


def first_products(count, rows, cols, tiles, source, acc, ready):
    spare, scen = acc.shape[0] - 1, acc.shape[1]
    live = count[0]
    acc[...] = jnp.zeros_like(acc)

    def part(first, size):
        ready(first)
        landing, results = [], []
        for g in range(first, first + size):
            landing.append(jnp.where(g < live, cols[g], spare))
        pair = 2 if size % 2 == 0 else 1
        for g in range(first, first + size, pair):
            picked = [source[rows[g + k]] for k in range(pair)]
            if pair == 2:
                blank = jnp.zeros_like(picked[0])
                left = jnp.concatenate(
                    [
                        jnp.concatenate([picked[0], blank], axis=1),
                        jnp.concatenate([blank, picked[1]], axis=1),
                    ],
                    axis=0,
                )
                right = jnp.concatenate([tiles[g], tiles[g + 1]], axis=0)
            else:
                left, right = picked[0], tiles[g]
            product = jnp.dot(left, right, preferred_element_type=jnp.float32)
            for k in range(pair):
                own = product[2 * scen * k : 2 * scen * (k + 1)]
                results.append(own[:scen] + own[scen:])
        for where, value in zip(landing, results):
            acc[where] += value

    over_parts(tiles, live, part)


def half_products(live, reads, lands, tiles, depth, source, acc):
    spare = acc.shape[0] - 1
    dims = (((1,), (depth,)), ((), ()))

    def part(first, size):
        landing, results = [], []
        for g in range(first, first + size):
            landing.append(jnp.where(g < live, lands(g), spare))
        pair = 2 if size % 2 == 0 else 1
        for g in range(first, first + size, pair):
            left = jnp.concatenate([source[k, reads(g + k)] for k in range(pair)], axis=1)
            right = jnp.concatenate([tiles[g + k] for k in range(pair)], axis=depth)
            product = lax.dot_general(left, right, dims, preferred_element_type=jnp.float32)
            rows = product.shape[0] // 2
            results += [product[rows * k : rows * (k + 1)] for k in range(pair)]
        for where, value in zip(landing, results):
            acc[where] += value

    over_parts(tiles, live, part, HALF_PARTS)


def put_source(source, k, quad):
    q, rows = source.shape[1] // 4, quad.shape[0] // 2
    high = quad.astype(jnp.bfloat16).astype(jnp.float32)
    low = quad - high
    for h in range(2):
        a, b = high[rows * h : rows * (h + 1)], low[rows * h : rows * (h + 1)]
        for j, block in ((0, upper_half(a, b)), (1, lower_half(a, b))):
            blank = jnp.zeros_like(block)
            where = k + (2 * h + j) * q
            source[0, where] = jnp.concatenate([block, blank], axis=0).astype(jnp.bfloat16)
            source[1, where] = jnp.concatenate([blank, block], axis=0).astype(jnp.bfloat16)


def pack(acc, out, norm, slot):
    q = (acc.shape[0] - 1) // 4
    for k in range(q):
        sums = [acc[k + j * q] for j in range(4)]
        sums = [value + turn_rows(value) for value in sums]
        halves = [jnp.where(top(sums[0].shape), sums[2 * h], sums[2 * h + 1]) for h in range(2)]
        out[k] = jnp.concatenate(halves, axis=0).astype(jnp.bfloat16)
    lanes = lax.broadcasted_iota(jnp.int32, acc.shape[1:], 1)
    out[q] = split_rows(jnp.where(lanes == slot, norm, 0.0))


def total_norm(parts):
    both = add_up([p[p.shape[0] - 1].astype(jnp.float32) for p in parts])
    rows = both.shape[0] // 2
    return jnp.sum(both[:rows] + both[rows:], axis=1, keepdims=True)


def partial_norm(squares):
    rows = squares.shape[0] // 2
    both = squares[:rows] + squares[rows:]
    return jnp.sum(both + turn_rows(both), axis=1, keepdims=True)


def quad_of_rows(array, k):
    q = array.shape[0] // 4
    rows = [array[k + j * q : k + j * q + 1, :] for j in range(4)]
    shape = (8, array.shape[1])
    return jnp.concatenate([jnp.where(top(shape), rows[2 * h], rows[2 * h + 1]) for h in range(2)], axis=0)


def pair_of_blocks(array, k, gap, odd):
    tile = 128
    a, b = (mine_first(array[:, n * tile : (n + 1) * tile], odd) for n in (k, k + gap))
    return upper_half(a, b), lower_half(a, b)


def is_odd():
    return lax.rem(lax.axis_index("rowblk"), 2) == 1


def first_kernel(*refs):
    count, rows_far, cols_far, tiles_far, dual_far, keep, send, tiles, rows, cols, source, acc, dual, sems = refs
    tile = tiles.shape[1]
    get_dual = pltpu.make_async_copy(dual_far, dual, sems.at[2])
    get_dual.start()
    copies = [
        pltpu.make_async_copy(rows_far, rows, sems.at[0]),
        pltpu.make_async_copy(cols_far, cols, sems.at[1]),
    ]
    for copy in copies:
        copy.start()
    get_tiles = {}
    for n, first in enumerate(range(0, tiles.shape[0], PART)):
        span = pl.ds(first, min(PART, tiles.shape[0] - first))
        get_tiles[first] = pltpu.make_async_copy(tiles_far.at[span], tiles.at[span], sems.at[3 + n])
        pl.when(first < count[0])(get_tiles[first].start)
    get_dual.wait()
    for b in range(source.shape[0]):
        source[b] = split_rows(dual[:, b * tile : (b + 1) * tile])
    for copy in copies:
        copy.wait()
    first_products(count, rows, cols, tiles, source, acc, lambda first: get_tiles[first].wait())
    odd = is_odd()
    q = keep.shape[0]
    for k in range(q):
        halves = []
        for h in range(2):
            a, b = (mine_first(acc[k + (2 * h + j) * q], odd) for j in range(2))
            halves.append((upper_half(a, b), lower_half(a, b)))
        keep[k] = jnp.concatenate([halves[0][0], halves[1][0]], axis=0)
        send[k] = jnp.concatenate([halves[0][1], halves[1][1]], axis=0).astype(jnp.bfloat16)


def turn_tiles(live, tiles, turned):
    def part(first, size):
        for g in range(first, first + size):
            turned[g] = tiles[g].T

    over_parts(tiles, live, part)


def turn_kernel(count, rows, cols, tiles, dual, demand, flag, after, turned, extra):
    del after
    total, half = rows.shape[1], flag.shape[0] // 2
    odd = is_odd()
    for k in range(half):
        extra[k] = pair_of_blocks(dual, k, half, odd)[1]
        extra[half + k] = pair_of_blocks(demand, k, half, odd)[1]
    for n in range(flag.shape[0] // 8):
        extra[2 * half + n] = flag[8 * n : 8 * (n + 1), :].astype(jnp.float32)
    last = extra.shape[0] - 1
    extra[last] = jnp.zeros(extra.shape[1:], jnp.float32)
    extra[last, 0:1, 0:total] = rows[...].astype(jnp.float32)
    extra[last, 1:2, 0:total] = cols[...].astype(jnp.float32)
    extra[last, 2:3, :] = jnp.full((1, extra.shape[2]), count[0], jnp.int32).astype(jnp.float32)
    turn_tiles(count[0], tiles, turned)


def col_kernel(begin, cost, upper, flag, after, start, price, limit):
    del after
    odd = is_odd()
    q = start.shape[0]
    for k in range(q):
        start[k] = jnp.concatenate([pair_of_blocks(begin, k + 2 * h * q, q, odd)[0] for h in range(2)], axis=0)
        price[k] = quad_of_rows(cost, k)
        limit[k] = jnp.where(quad_of_rows(flag, k) > 0, quad_of_rows(upper, k), jnp.inf)


def row_kernel(extra, demand, flag, begin, after, start, right, floor):
    del after
    odd = is_odd()
    half, tile = start.shape[0], start.shape[2]
    for k in range(half):
        start[k] = jnp.concatenate([pair_of_blocks(begin, k, half, odd)[0], extra[k]], axis=0)
        right[k] = jnp.concatenate([pair_of_blocks(demand, k, half, odd)[0], extra[half + k]], axis=0)
        own = [flag[n : n + 1, :].astype(jnp.float32) for n in (k, k + half)]
        far = [extra[2 * half + n // 8, n % 8 : n % 8 + 1, :] for n in (k, k + half)]
        marks = [jnp.where(top((8, tile)), a, b) for a, b in (own, far)]
        floor[k] = jnp.where(jnp.concatenate(marks, axis=0) > 0.0, 0.0, -jnp.inf)


def turn_other_kernel(grid, tiles, after, turned):
    del after
    turn_tiles(grid[2, 0], tiles, turned)


def primal_kernel(mix, last, n_parts, *refs):
    count, rows, cols, tiles, other = refs[:5]
    parts = refs[5 : 5 + n_parts]
    price, limit, start, *refs = refs[5 + n_parts :]
    if last:
        grid, weight_in, primal_norm, point, point_out, weight_out, out, source, acc = refs
        dual_norm = total_norm(parts)
        weight = weight_in[:, :1]
        ratio = (dual_norm + EPS) / (primal_norm[:, :1] + EPS)
        weight = jnp.sqrt(weight * jnp.sqrt(ratio))
        weight_out[...] = jnp.broadcast_to(weight, weight_out.shape)
    else:
        extra, point_out, out, grid, source, acc, whole, sem = refs
        point = start
        whole[...] = extra[extra.shape[0] - 1].astype(jnp.int32)
        get_grid = pltpu.make_async_copy(whole, grid, sem)
        get_grid.start()
        weight = jnp.ones((8, 1), jnp.float32)
    q = point_out.shape[0]
    tile = point_out.shape[2]
    tau = jnp.broadcast_to(ETA / weight, (weight.shape[0], tile))
    tau = jnp.concatenate([tau, tau], axis=0)
    squares = jnp.zeros_like(tau)
    for k in range(q):
        value = add_up([p[k].astype(jnp.float32) for p in parts])
        old = point[k]
        moved = old - tau * (price[k] - value)
        x_hat = jnp.maximum(jnp.minimum(moved, limit[k]), 0.0)
        step = x_hat - old
        squares += step * step
        x_bar = 2.0 * x_hat - old
        point_out[k] = mix * x_bar + (1.0 - mix) * start[k]
        put_source(source, k, x_bar)
    acc[...] = jnp.zeros_like(acc)
    near = (acc.shape[0] - 1) // 2
    half_products(count[0], lambda g: cols[g], lambda g: rows[g], tiles, 0, source, acc)
    if not last:
        get_grid.wait()
    half_products(grid[2, 0], lambda g: grid[1, g], lambda g: near + grid[0, g], other, 0 if last else 1, source, acc)
    pack(acc, out, partial_norm(squares), lax.axis_index("colblk"))


def dual_kernel(mix, last, n_parts, *refs):
    if last:
        parts = refs[:n_parts]
        refs = refs[n_parts:]
        weight, start, right, floor, dual, keep, send, small = refs
    else:
        count, rows, cols, grid, tiles, other = refs[:6]
        parts = refs[6 : 6 + n_parts]
        refs = refs[6 + n_parts :]
        weight, start, right, floor, dual_out, primal_norm, out, source, acc = refs
        dual = start
    if n_parts == 4:
        parts = [parts[0], parts[2], parts[1], parts[3]]
    primal_total = total_norm(parts)
    sigma = jnp.concatenate([ETA * weight[...]] * 2, axis=0)
    squares = jnp.zeros_like(sigma)
    for k in range(start.shape[0]):
        value = add_up([p[k].astype(jnp.float32) for p in parts])
        old = dual[k]
        moved = old + sigma * (right[k] - value)
        y_hat = jnp.maximum(moved, floor[k])
        step = y_hat - old
        squares += step * step
        new = mix * (2.0 * y_hat - old) + (1.0 - mix) * start[k]
        if last:
            keep[k] = new[:8]
            send[k] = new[8:]
        else:
            dual_out[k] = new
            put_source(source, k, new)
    dual_norm = partial_norm(squares)
    if last:
        lanes = lax.broadcasted_iota(jnp.int32, small.shape, 1)
        first = jnp.where(is_odd(), 3, 0)
        values = jnp.where(lanes == first, dual_norm, 0.0)
        values = jnp.where(lanes == first + 1, primal_total, values)
        small[...] = jnp.where(lanes == first + 2, weight[...], values)
    else:
        primal_norm[...] = jnp.broadcast_to(primal_total, primal_norm.shape)
        acc[...] = jnp.zeros_like(acc)
        near = source.shape[1] // 2
        half_products(count[0], lambda g: rows[g], lambda g: cols[g], tiles, 0, source, acc)
        half_products(grid[2, 0], lambda g: near + grid[0, g], lambda g: grid[1, g], other, 0, source, acc)
        pack(acc, out, dual_norm, lax.axis_index("rowblk"))


def join(mine, others, out):
    tile = mine.shape[2]
    odd = is_odd()
    q, pairs = mine.shape[0], mine.shape[1] // 8
    for k in range(q):
        for h in range(pairs):
            a, b = mine[k, 8 * h : 8 * (h + 1), :], others[k, 8 * h : 8 * (h + 1), :]
            a, b = jnp.where(odd, b, a), jnp.where(odd, a, b)
            for j, value in ((0, upper_half(a, b)), (1, lower_half(a, b))):
                n = k + (2 * h + j) * q
                out[:, n * tile : (n + 1) * tile] = value


def end_kernel(share, *refs):
    mine_x, other_x, mine_y, other_y, *parts = refs[:-7]
    far_x, far_y, far_weight, x_out, y_out, weight_out, sems = refs[-7:]
    copies = []
    for n, (mine, others, out, target) in enumerate(((mine_x, other_x, x_out, far_x), (mine_y, other_y, y_out, far_y))):
        join(mine, others, out)
        copies.append(pltpu.make_async_copy(out, target, sems.at[n]))
        copies[-1].start()
    both = add_up([p[...] for p in parts])
    found = []
    for first in (0, 3):
        dual_norm, primal_norm, weight = (both[:, first + n : first + n + 1] for n in range(3))
        ratio = (dual_norm + EPS) / (primal_norm * share + EPS)
        found.append(jnp.sqrt(weight * share * jnp.sqrt(ratio)))
    weight = jnp.where(top(found[0].shape), found[0], found[1])
    lanes, rows = (lax.broadcasted_iota(jnp.int32, both.shape, n) for n in (1, 0))
    row = jnp.sum(jnp.where(lanes == rows, weight, 0.0), axis=0, keepdims=True)
    weight_out[...] = row[:, : weight_out.shape[1]]
    copies.append(pltpu.make_async_copy(weight_out, far_weight, sems.at[2]))
    copies[-1].start()
    for copy in copies:
        copy.wait()


def call(kernel, inputs, in_specs, outputs, out_specs, scratch, cost=None):
    return pl.pallas_call(
        kernel,
        out_shape=outputs,
        in_specs=in_specs,
        out_specs=out_specs,
        scratch_shapes=scratch,
        cost_estimate=cost,
        compiler_params=pltpu.CompilerParams(vmem_limit_bytes=VMEM_LIMIT),
    )(*inputs)


def far(value):
    return pltpu.with_memory_space_constraint(value, pltpu.HBM)


def swap(value, axis, mask):
    size = lax.axis_size(axis)
    return lax.ppermute(value, axis, [(i, i ^ mask) for i in range(size)])


def butterfly(value, axis, radix, mask=1):
    size = lax.axis_size(axis)
    parts = [value]
    while mask < size:
        total = add_up([p.astype(jnp.float32) for p in parts]).astype(value.dtype)
        span = min(radix, size // mask)
        parts = [total] + [swap(total, axis, mask * k) for k in range(1, span)]
        mask *= span
    return parts


def on_device(
    tiles,
    tile_row,
    tile_col,
    tile_count,
    cost,
    demand,
    upper,
    col_flag,
    row_flag,
    primal_start,
    dual_start,
):
    tile = tiles.shape[1]
    total = tile_row.shape[0]
    scen = primal_start.shape[0]
    col_blocks = primal_start.shape[1] // tile
    row_blocks = dual_start.shape[1] // tile
    bf16, f32, i32 = jnp.bfloat16, jnp.float32, jnp.int32
    cost, upper, col_flag = (v.reshape(col_blocks, tile) for v in (cost, upper, col_flag))
    row_flag = row_flag.reshape(row_blocks, tile)

    small = pltpu.VMEM((scen, tile), f32)
    col_quads, row_quads = col_blocks // 4, row_blocks // 2
    col_state = pltpu.VMEM((col_quads, 2 * scen, tile), f32)
    row_state = pltpu.VMEM((row_quads, 2 * scen, tile), f32)
    row_half = pltpu.VMEM((row_quads, scen, tile), f32)
    col_terms = pltpu.VMEM((col_quads + 1, 2 * scen, tile), bf16)
    row_terms = pltpu.VMEM((row_quads + 1, 2 * scen, tile), bf16)
    tiles_like = pltpu.VMEM(tiles.shape, tiles.dtype)
    index = pltpu.SMEM((total,), i32)
    to_cols = [
        pltpu.VMEM((2, 2 * row_blocks, 2 * scen, tile), bf16),
        pltpu.VMEM((col_blocks + 1, scen, tile), f32),
    ]
    to_rows = [
        pltpu.VMEM((2, col_blocks, 2 * scen, tile), bf16),
        pltpu.VMEM((2 * row_blocks + 1, scen, tile), f32),
    ]
    turning = pl.CostEstimate(flops=0, bytes_accessed=2 * tiles.size * 2, transcendentals=0)

    keep, send, tiles, rows, cols = call(
        first_kernel,
        [tile_count, far(tile_row), far(tile_col), far(tiles), far(dual_start)],
        [SMEM_SPEC] + [FAR_SPEC] * 4,
        [col_state, pltpu.VMEM((col_quads, 2 * scen, tile), bf16), tiles_like, index, index],
        [VMEM_SPEC] * 3 + [SMEM_SPEC] * 2,
        [
            pltpu.VMEM((row_blocks, 2 * scen, tile), bf16),
            pltpu.VMEM((col_blocks + 1, scen, tile), f32),
            pltpu.VMEM(dual_start.shape, f32),
            pltpu.SemaphoreType.DMA((3 + pl.cdiv(total, PART),)),
        ],
    )
    terms = (keep + swap(send, "rowblk", 1).astype(f32)).astype(bf16)
    held_tiles, terms = lax.optimization_barrier((tiles, terms))
    parts = butterfly(terms, "rowblk", 2, 2)
    other = swap(held_tiles, "rowblk", 1)
    turned, extra = call(
        turn_kernel,
        [tile_count, tile_row.reshape(1, total), tile_col.reshape(1, total), tiles, dual_start, demand, row_flag, terms],
        [SMEM_SPEC] + [VMEM_SPEC] * 7,
        [tiles_like, pltpu.VMEM((2 * row_quads + row_blocks // 8 + 1, scen, tile), f32)],
        [VMEM_SPEC] * 2,
        [],
        turning,
    )
    extra = swap(extra, "rowblk", 1)
    columns = call(
        col_kernel,
        [primal_start, cost, upper, col_flag, terms],
        [VMEM_SPEC] * 5,
        [col_state] * 3,
        [VMEM_SPEC] * 3,
        [],
    )
    start, price, limit = columns
    own = [tile_count, rows, cols]
    weight = jnp.ones((scen, tile), f32)
    for step in range(ITERS):
        mix = (step + 1.0) / (step + 2.0)
        last = step == ITERS - 1
        if step:
            parts = butterfly(terms, "rowblk", 2, 2)
            (other_turned,) = call(
                turn_other_kernel,
                [grid, other, terms],
                [SMEM_SPEC] + [VMEM_SPEC] * 2,
                [tiles_like],
                [VMEM_SPEC],
                [],
                turning,
            )
            vectors = [*parts, price, limit, start]
            point, weight, terms = call(
                functools.partial(primal_kernel, mix, True, len(parts)),
                [*own, turned, other_turned, *vectors, grid, weight, primal_norm, point],
                [SMEM_SPEC] * 3 + [VMEM_SPEC] * (2 + len(vectors)) + [SMEM_SPEC] + [VMEM_SPEC] * 3,
                [col_state, small, row_terms],
                [VMEM_SPEC] * 3,
                to_rows,
            )
        else:
            vectors = [*parts, price, limit, start, extra]
            point, terms, grid = call(
                functools.partial(primal_kernel, mix, False, len(parts)),
                [*own, turned, other, *vectors],
                [SMEM_SPEC] * 3 + [VMEM_SPEC] * (2 + len(vectors)),
                [col_state, row_terms, pltpu.SMEM((scen, tile), i32)],
                [VMEM_SPEC] * 2 + [SMEM_SPEC],
                [*to_rows, pltpu.VMEM((scen, tile), i32), pltpu.SemaphoreType.DMA],
            )
        parts = butterfly(terms, "colblk", 4)
        if len(parts) == 4:
            parts = [parts[n] for n in (0, 2, 1, 3)]
        if step == 0:
            lines = call(
                row_kernel,
                [extra, demand, row_flag, dual_start, terms],
                [VMEM_SPEC] * 5,
                [row_state] * 3,
                [VMEM_SPEC] * 3,
                [],
            )
        vectors = [*parts, weight, *lines]
        if last:
            keep, send, terms = call(
                functools.partial(dual_kernel, mix, True, len(parts)),
                [*vectors, dual],
                [VMEM_SPEC] * (1 + len(vectors)),
                [row_half, row_half, small],
                [VMEM_SPEC] * 3,
                [],
            )
        else:
            dual, primal_norm, terms = call(
                functools.partial(dual_kernel, mix, False, len(parts)),
                [*own, grid, tiles, other, *vectors],
                [SMEM_SPEC] * 4 + [VMEM_SPEC] * (2 + len(vectors)),
                [row_state, small, col_terms],
                [VMEM_SPEC] * 3,
                to_cols,
            )
    point, terms = lax.optimization_barrier((point, terms))
    parts = butterfly(terms, "rowblk", 4)
    halves = [point, swap(point, "rowblk", 1), keep, swap(send, "rowblk", 1)]
    shapes = [primal_start.shape, dual_start.shape, (1, scen)]
    point, dual, weight = call(
        functools.partial(end_kernel, 2.0 / lax.axis_size("rowblk")),
        [*halves, *parts],
        [VMEM_SPEC] * (4 + len(parts)),
        [jax.ShapeDtypeStruct(shape, f32) for shape in shapes],
        [FAR_SPEC] * 3,
        [pltpu.VMEM(shape, f32) for shape in shapes] + [pltpu.SemaphoreType.DMA((3,))],
    )
    return point, dual, weight.reshape(scen)


def solution(mesh):
    return jax.shard_map(
        on_device,
        mesh=mesh,
        in_specs=(
            P(("groups", "rowblk", "colblk"), None, None),
            P(("groups", "rowblk", "colblk")),
            P(("groups", "rowblk", "colblk")),
            P(("groups", "rowblk", "colblk")),
            P(("groups", "colblk")),
            P(None, ("groups", "rowblk")),
            P(("groups", "colblk")),
            P(("groups", "colblk")),
            P(("groups", "rowblk")),
            P(None, ("groups", "colblk")),
            P(None, ("groups", "rowblk")),
        ),
        out_specs=(P(None, ("groups", "colblk")), P(None, ("groups", "rowblk")), P("groups")),
        check_vma=False,
    )
```

```python
import functools

import jax
import jax.numpy as jnp
from jax import lax
from jax.experimental import pallas as pl
from jax.experimental.pallas import tpu as pltpu
from jax.sharding import PartitionSpec as P

ITERS = 2
ETA = 0.3
EPS = 1e-06
PART = 24
HALF_PARTS = (32, 16, 24)
VMEM_LIMIT = 8 * 1024 * 1024

SMEM_SPEC = pl.BlockSpec(memory_space=pltpu.SMEM)
VMEM_SPEC = pl.BlockSpec(memory_space=pltpu.VMEM)
FAR_SPEC = pl.BlockSpec(memory_space=pltpu.HBM)


def top(shape):
    return lax.broadcasted_iota(jnp.int32, shape, 0) < shape[0] // 2


def turn_rows(value):
    return pltpu.roll(value, value.shape[0] // 2, 0)


def upper_half(a, b):
    return jnp.where(top(a.shape), a, turn_rows(b))


def lower_half(a, b):
    return jnp.where(top(a.shape), turn_rows(a), b)


def mine_first(value, odd):
    return jnp.where(odd, turn_rows(value), value)


def split_rows(value):
    high = value.astype(jnp.bfloat16)
    low = (value - high.astype(jnp.float32)).astype(jnp.bfloat16)
    return jnp.concatenate([high, low], axis=0)


def add_up(terms):
    while len(terms) > 1:
        terms = [terms[i] + terms[i + 1] for i in range(0, len(terms), 2)]
    return terms[0]


def over_parts(tiles, live, part, sizes=(PART,)):
    total, first, n = tiles.shape[0], 0, 0
    while first < total:
        size = min(sizes[min(n, len(sizes) - 1)], total - first)
        pl.when(first < live)(functools.partial(part, first, size))
        first, n = first + size, n + 1


def first_products(count, rows, cols, tiles, source, acc, ready):
    spare, scen = acc.shape[0] - 1, acc.shape[1]
    live = count[0]
    acc[...] = jnp.zeros_like(acc)

    def part(first, size):
        ready(first)
        landing, results = [], []
        for g in range(first, first + size):
            landing.append(jnp.where(g < live, cols[g], spare))
        pair = 2 if size % 2 == 0 else 1
        for g in range(first, first + size, pair):
            picked = [source[rows[g + k]] for k in range(pair)]
            if pair == 2:
                blank = jnp.zeros_like(picked[0])
                left = jnp.concatenate(
                    [
                        jnp.concatenate([picked[0], blank], axis=1),
                        jnp.concatenate([blank, picked[1]], axis=1),
                    ],
                    axis=0,
                )
                right = jnp.concatenate([tiles[g], tiles[g + 1]], axis=0)
            else:
                left, right = picked[0], tiles[g]
            product = jnp.dot(left, right, preferred_element_type=jnp.float32)
            for k in range(pair):
                own = product[2 * scen * k : 2 * scen * (k + 1)]
                results.append(own[:scen] + own[scen:])
        for where, value in zip(landing, results):
            acc[where] += value

    over_parts(tiles, live, part)


def half_products(live, reads, lands, tiles, depth, source, acc):
    spare = acc.shape[0] - 1
    dims = (((1,), (depth,)), ((), ()))

    def part(first, size):
        landing, results = [], []
        for g in range(first, first + size):
            landing.append(jnp.where(g < live, lands(g), spare))
        pair = 2 if size % 2 == 0 else 1
        for g in range(first, first + size, pair):
            left = jnp.concatenate([source[k, reads(g + k)] for k in range(pair)], axis=1)
            right = jnp.concatenate([tiles[g + k] for k in range(pair)], axis=depth)
            product = lax.dot_general(left, right, dims, preferred_element_type=jnp.float32)
            rows = product.shape[0] // 2
            results += [product[rows * k : rows * (k + 1)] for k in range(pair)]
        for where, value in zip(landing, results):
            acc[where] += value

    over_parts(tiles, live, part, HALF_PARTS)


def put_source(source, k, quad):
    q, rows = source.shape[1] // 4, quad.shape[0] // 2
    high = quad.astype(jnp.bfloat16).astype(jnp.float32)
    low = quad - high
    for h in range(2):
        a, b = high[rows * h : rows * (h + 1)], low[rows * h : rows * (h + 1)]
        for j, block in ((0, upper_half(a, b)), (1, lower_half(a, b))):
            blank = jnp.zeros_like(block)
            where = k + (2 * h + j) * q
            source[0, where] = jnp.concatenate([block, blank], axis=0).astype(jnp.bfloat16)
            source[1, where] = jnp.concatenate([blank, block], axis=0).astype(jnp.bfloat16)


def pack(acc, out, norm, slot):
    q = (acc.shape[0] - 1) // 4
    for k in range(q):
        sums = [acc[k + j * q] for j in range(4)]
        sums = [value + turn_rows(value) for value in sums]
        halves = [jnp.where(top(sums[0].shape), sums[2 * h], sums[2 * h + 1]) for h in range(2)]
        out[k] = jnp.concatenate(halves, axis=0).astype(jnp.bfloat16)
    lanes = lax.broadcasted_iota(jnp.int32, acc.shape[1:], 1)
    out[q] = split_rows(jnp.where(lanes == slot, norm, 0.0))


def total_norm(parts):
    both = add_up([p[p.shape[0] - 1].astype(jnp.float32) for p in parts])
    rows = both.shape[0] // 2
    return jnp.sum(both[:rows] + both[rows:], axis=1, keepdims=True)


def partial_norm(squares):
    rows = squares.shape[0] // 2
    both = squares[:rows] + squares[rows:]
    return jnp.sum(both + turn_rows(both), axis=1, keepdims=True)


def quad_of_rows(array, k):
    q = array.shape[0] // 4
    rows = [array[k + j * q : k + j * q + 1, :] for j in range(4)]
    shape = (8, array.shape[1])
    return jnp.concatenate([jnp.where(top(shape), rows[2 * h], rows[2 * h + 1]) for h in range(2)], axis=0)


def pair_of_blocks(array, k, gap, odd):
    tile = 128
    a, b = (mine_first(array[:, n * tile : (n + 1) * tile], odd) for n in (k, k + gap))
    return upper_half(a, b), lower_half(a, b)


def is_odd():
    return lax.rem(lax.axis_index("rowblk"), 2) == 1


def grid_lines(count, rows, cols, shape):
    lanes, lines = (lax.broadcasted_iota(jnp.int32, (shape[0] // 2, shape[1]), n) for n in (1, 0))
    ways = 4
    found = []
    for index in (rows, cols):
        terms = [jnp.zeros(lanes.shape, jnp.int32)] * ways
        for g in range(index.shape[0]):
            terms[g % ways] = jnp.where(lanes == g, index[g], terms[g % ways])
        found.append(add_up(terms))
    both = jnp.where(lines == 0, found[0], jnp.where(lines == 1, found[1], count[0]))
    both = both.astype(jnp.float32)
    return jnp.concatenate([both, jnp.zeros_like(both)], axis=0).astype(jnp.bfloat16)


def first_kernel(*refs):
    count, rows_far, cols_far, tiles_far, dual_far, keep, send, tiles, rows, cols, source, acc, dual, sems = refs
    tile = tiles.shape[1]
    get_dual = pltpu.make_async_copy(dual_far, dual, sems.at[2])
    get_dual.start()
    copies = [
        pltpu.make_async_copy(rows_far, rows, sems.at[0]),
        pltpu.make_async_copy(cols_far, cols, sems.at[1]),
    ]
    for copy in copies:
        copy.start()
    get_tiles = {}
    for n, first in enumerate(range(0, tiles.shape[0], PART)):
        span = pl.ds(first, min(PART, tiles.shape[0] - first))
        get_tiles[first] = pltpu.make_async_copy(tiles_far.at[span], tiles.at[span], sems.at[3 + n])
        pl.when(first < count[0])(get_tiles[first].start)
    get_dual.wait()
    for b in range(source.shape[0]):
        source[b] = split_rows(dual[:, b * tile : (b + 1) * tile])
    for copy in copies:
        copy.wait()
    lines = grid_lines(count, rows, cols, send.shape[1:])
    first_products(count, rows, cols, tiles, source, acc, lambda first: get_tiles[first].wait())
    odd = is_odd()
    q = keep.shape[0]
    for k in range(q):
        halves = []
        for h in range(2):
            a, b = (mine_first(acc[k + (2 * h + j) * q], odd) for j in range(2))
            halves.append((upper_half(a, b), lower_half(a, b)))
        keep[k] = jnp.concatenate([halves[0][0], halves[1][0]], axis=0)
        send[k] = jnp.concatenate([halves[0][1], halves[1][1]], axis=0).astype(jnp.bfloat16)
    send[q] = lines


def turn_tiles(live, tiles, turned):
    def part(first, size):
        for g in range(first, first + size):
            turned[g] = tiles[g].T

    over_parts(tiles, live, part)


def turn_kernel(count, tiles, after, turned):
    del after
    turn_tiles(count[0], tiles, turned)


def extra_kernel(dual, demand, flag, after, extra):
    del after
    half = flag.shape[0] // 2
    odd = is_odd()
    for k in range(half):
        extra[k] = pair_of_blocks(dual, k, half, odd)[1]
        extra[half + k] = pair_of_blocks(demand, k, half, odd)[1]
    for n in range(flag.shape[0] // 8):
        extra[2 * half + n] = flag[8 * n : 8 * (n + 1), :].astype(jnp.float32)


def grid_kernel(received, after, grid, whole, sem):
    del after
    last = received[received.shape[0] - 1].astype(jnp.float32)
    whole[...] = last[: whole.shape[0]].astype(jnp.int32)
    copy = pltpu.make_async_copy(whole, grid, sem)
    copy.start()
    copy.wait()


def col_kernel(begin, cost, upper, flag, after, start, price, limit):
    del after
    odd = is_odd()
    q = start.shape[0]
    for k in range(q):
        start[k] = jnp.concatenate([pair_of_blocks(begin, k + 2 * h * q, q, odd)[0] for h in range(2)], axis=0)
        price[k] = quad_of_rows(cost, k)
        limit[k] = jnp.where(quad_of_rows(flag, k) > 0, quad_of_rows(upper, k), jnp.inf)


def row_kernel(extra, demand, flag, begin, after, start, right, floor):
    del after
    odd = is_odd()
    half, tile = start.shape[0], start.shape[2]
    for k in range(half):
        start[k] = jnp.concatenate([pair_of_blocks(begin, k, half, odd)[0], extra[k]], axis=0)
        right[k] = jnp.concatenate([pair_of_blocks(demand, k, half, odd)[0], extra[half + k]], axis=0)
        own = [flag[n : n + 1, :].astype(jnp.float32) for n in (k, k + half)]
        far = [extra[2 * half + n // 8, n % 8 : n % 8 + 1, :] for n in (k, k + half)]
        marks = [jnp.where(top((8, tile)), a, b) for a, b in (own, far)]
        floor[k] = jnp.where(jnp.concatenate(marks, axis=0) > 0.0, 0.0, -jnp.inf)


def turn_other_kernel(grid, tiles, after, turned):
    del after
    turn_tiles(grid[2, 0], tiles, turned)


def primal_kernel(mix, last, n_parts, *refs):
    count, rows, cols, tiles, other = refs[:5]
    parts = refs[5 : 5 + n_parts]
    price, limit, start, *refs = refs[5 + n_parts :]
    if last:
        grid, weight_in, primal_norm, point, point_out, weight_out, out, source, acc = refs
        dual_norm = total_norm(parts)
        weight = weight_in[:, :1]
        ratio = (dual_norm + EPS) / (primal_norm[:, :1] + EPS)
        weight = jnp.sqrt(weight * jnp.sqrt(ratio))
        weight_out[...] = jnp.broadcast_to(weight, weight_out.shape)
    else:
        grid, point_out, out, source, acc = refs
        point = start
        weight = jnp.ones((8, 1), jnp.float32)
    q = point_out.shape[0]
    tile = point_out.shape[2]
    tau = jnp.broadcast_to(ETA / weight, (weight.shape[0], tile))
    tau = jnp.concatenate([tau, tau], axis=0)
    squares = jnp.zeros_like(tau)
    for k in range(q):
        value = add_up([p[k].astype(jnp.float32) for p in parts])
        old = point[k]
        moved = old - tau * (price[k] - value)
        x_hat = jnp.maximum(jnp.minimum(moved, limit[k]), 0.0)
        step = x_hat - old
        squares += step * step
        x_bar = 2.0 * x_hat - old
        point_out[k] = mix * x_bar + (1.0 - mix) * start[k]
        put_source(source, k, x_bar)
    acc[...] = jnp.zeros_like(acc)
    near = (acc.shape[0] - 1) // 2
    half_products(count[0], lambda g: cols[g], lambda g: rows[g], tiles, 0, source, acc)
    half_products(grid[2, 0], lambda g: grid[1, g], lambda g: near + grid[0, g], other, 0 if last else 1, source, acc)
    pack(acc, out, partial_norm(squares), lax.axis_index("colblk"))


def dual_kernel(mix, last, n_parts, *refs):
    if last:
        parts = refs[:n_parts]
        refs = refs[n_parts:]
        weight, start, right, floor, dual, keep, send, small = refs
    else:
        count, rows, cols, grid, tiles, other = refs[:6]
        parts = refs[6 : 6 + n_parts]
        refs = refs[6 + n_parts :]
        weight, start, right, floor, dual_out, primal_norm, out, source, acc = refs
        dual = start
    if n_parts == 4:
        parts = [parts[0], parts[2], parts[1], parts[3]]
    primal_total = total_norm(parts)
    sigma = jnp.concatenate([ETA * weight[...]] * 2, axis=0)
    squares = jnp.zeros_like(sigma)
    for k in range(start.shape[0]):
        value = add_up([p[k].astype(jnp.float32) for p in parts])
        old = dual[k]
        moved = old + sigma * (right[k] - value)
        y_hat = jnp.maximum(moved, floor[k])
        step = y_hat - old
        squares += step * step
        new = mix * (2.0 * y_hat - old) + (1.0 - mix) * start[k]
        if last:
            keep[k] = new[:8]
            send[k] = new[8:]
        else:
            dual_out[k] = new
            put_source(source, k, new)
    dual_norm = partial_norm(squares)
    if last:
        lanes = lax.broadcasted_iota(jnp.int32, small.shape, 1)
        first = jnp.where(is_odd(), 3, 0)
        values = jnp.where(lanes == first, dual_norm, 0.0)
        values = jnp.where(lanes == first + 1, primal_total, values)
        small[...] = jnp.where(lanes == first + 2, weight[...], values)
    else:
        primal_norm[...] = jnp.broadcast_to(primal_total, primal_norm.shape)
        acc[...] = jnp.zeros_like(acc)
        near = source.shape[1] // 2
        half_products(count[0], lambda g: rows[g], lambda g: cols[g], tiles, 0, source, acc)
        half_products(grid[2, 0], lambda g: near + grid[0, g], lambda g: grid[1, g], other, 0, source, acc)
        pack(acc, out, dual_norm, lax.axis_index("rowblk"))


def join(mine, others, out):
    tile = mine.shape[2]
    odd = is_odd()
    q, pairs = mine.shape[0], mine.shape[1] // 8
    for k in range(q):
        for h in range(pairs):
            a, b = mine[k, 8 * h : 8 * (h + 1), :], others(k, h)
            a, b = jnp.where(odd, b, a), jnp.where(odd, a, b)
            for j, value in ((0, upper_half(a, b)), (1, lower_half(a, b))):
                n = k + (2 * h + j) * q
                out[:, n * tile : (n + 1) * tile] = value


def gather_kernel(point, send, both):
    q = point.shape[0]
    both[:q] = point[...]
    for k in range(send.shape[0] // 2):
        both[q + k] = jnp.concatenate([send[2 * k], send[2 * k + 1]], axis=0)


def result_kernel(mine_x, mine_y, other, far_x, far_y, x_out, y_out, sems):
    copies = []
    q = mine_x.shape[0]
    from_x = lambda k, h: other[k, 8 * h : 8 * (h + 1), :]
    from_y = lambda k, h: other[q + k // 2, 8 * (k % 2) : 8 * (k % 2 + 1), :]
    for n, (mine, others, out, target) in enumerate(((mine_x, from_x, x_out, far_x), (mine_y, from_y, y_out, far_y))):
        join(mine, others, out)
        copies.append(pltpu.make_async_copy(out, target, sems.at[n]))
        copies[-1].start()
    for copy in copies:
        copy.wait()


def weight_kernel(share, *refs):
    *parts, after, out = refs
    del after
    both = add_up([p[...] for p in parts])
    found = []
    for first in (0, 3):
        dual_norm, primal_norm, weight = (both[:, first + n : first + n + 1] for n in range(3))
        ratio = (dual_norm + EPS) / (primal_norm * share + EPS)
        found.append(jnp.sqrt(weight * share * jnp.sqrt(ratio)))
    weight = jnp.where(top(found[0].shape), found[0], found[1])
    lanes, rows = (lax.broadcasted_iota(jnp.int32, both.shape, n) for n in (1, 0))
    row = jnp.sum(jnp.where(lanes == rows, weight, 0.0), axis=0, keepdims=True)
    out[...] = row[:, : out.shape[1]]


def call(kernel, inputs, in_specs, outputs, out_specs, scratch, cost=None):
    return pl.pallas_call(
        kernel,
        out_shape=outputs,
        in_specs=in_specs,
        out_specs=out_specs,
        scratch_shapes=scratch,
        cost_estimate=cost,
        compiler_params=pltpu.CompilerParams(vmem_limit_bytes=VMEM_LIMIT),
    )(*inputs)


def far(value):
    return pltpu.with_memory_space_constraint(value, pltpu.HBM)


def swap(value, axis, mask):
    size = lax.axis_size(axis)
    return lax.ppermute(value, axis, [(i, i ^ mask) for i in range(size)])


def butterfly(value, axis, radix, mask=1):
    size = lax.axis_size(axis)
    parts = [value]
    while mask < size:
        total = add_up([p.astype(jnp.float32) for p in parts]).astype(value.dtype)
        span = min(radix, size // mask)
        parts = [total] + [swap(total, axis, mask * k) for k in range(1, span)]
        mask *= span
    return parts


def on_device(
    tiles,
    tile_row,
    tile_col,
    tile_count,
    cost,
    demand,
    upper,
    col_flag,
    row_flag,
    primal_start,
    dual_start,
):
    tile = tiles.shape[1]
    total = tile_row.shape[0]
    scen = primal_start.shape[0]
    col_blocks = primal_start.shape[1] // tile
    row_blocks = dual_start.shape[1] // tile
    bf16, f32, i32 = jnp.bfloat16, jnp.float32, jnp.int32
    cost, upper, col_flag = (v.reshape(col_blocks, tile) for v in (cost, upper, col_flag))
    row_flag = row_flag.reshape(row_blocks, tile)

    small = pltpu.VMEM((scen, tile), f32)
    col_quads, row_quads = col_blocks // 4, row_blocks // 2
    col_state = pltpu.VMEM((col_quads, 2 * scen, tile), f32)
    row_state = pltpu.VMEM((row_quads, 2 * scen, tile), f32)
    row_half = pltpu.VMEM((row_quads, scen, tile), f32)
    col_terms = pltpu.VMEM((col_quads + 1, 2 * scen, tile), bf16)
    row_terms = pltpu.VMEM((row_quads + 1, 2 * scen, tile), bf16)
    tiles_like = pltpu.VMEM(tiles.shape, tiles.dtype)
    index = pltpu.SMEM((total,), i32)
    to_cols = [
        pltpu.VMEM((2, 2 * row_blocks, 2 * scen, tile), bf16),
        pltpu.VMEM((col_blocks + 1, scen, tile), f32),
    ]
    to_rows = [
        pltpu.VMEM((2, col_blocks, 2 * scen, tile), bf16),
        pltpu.VMEM((2 * row_blocks + 1, scen, tile), f32),
    ]
    turning = pl.CostEstimate(flops=0, bytes_accessed=2 * tiles.size * 2, transcendentals=0)

    keep, send, tiles, rows, cols = call(
        first_kernel,
        [tile_count, far(tile_row), far(tile_col), far(tiles), far(dual_start)],
        [SMEM_SPEC] + [FAR_SPEC] * 4,
        [col_state, col_terms, tiles_like, index, index],
        [VMEM_SPEC] * 3 + [SMEM_SPEC] * 2,
        [
            pltpu.VMEM((row_blocks, 2 * scen, tile), bf16),
            pltpu.VMEM((col_blocks + 1, scen, tile), f32),
            pltpu.VMEM(dual_start.shape, f32),
            pltpu.SemaphoreType.DMA((3 + pl.cdiv(total, PART),)),
        ],
    )
    received = swap(send, "rowblk", 1)
    terms = (keep + received[:col_quads].astype(f32)).astype(bf16)
    held_tiles, terms = lax.optimization_barrier((tiles, terms))
    parts = butterfly(terms, "rowblk", 2, 2)
    other = swap(held_tiles, "rowblk", 1)
    (turned,) = call(
        turn_kernel,
        [tile_count, tiles, terms],
        [SMEM_SPEC] + [VMEM_SPEC] * 2,
        [tiles_like],
        [VMEM_SPEC],
        [],
        turning,
    )
    (extra,) = call(
        extra_kernel,
        [dual_start, demand, row_flag, terms],
        [VMEM_SPEC] * 4,
        [pltpu.VMEM((2 * row_quads + row_blocks // 8, scen, tile), f32)],
        [VMEM_SPEC],
        [],
    )
    extra = swap(extra, "rowblk", 1)
    columns = call(
        col_kernel,
        [primal_start, cost, upper, col_flag, terms],
        [VMEM_SPEC] * 5,
        [col_state] * 3,
        [VMEM_SPEC] * 3,
        [],
    )
    start, price, limit = columns
    (grid,) = call(
        grid_kernel,
        [received, terms],
        [VMEM_SPEC] * 2,
        [pltpu.SMEM((scen, tile), i32)],
        [SMEM_SPEC],
        [pltpu.VMEM((scen, tile), i32), pltpu.SemaphoreType.DMA],
    )
    own = [tile_count, rows, cols]
    weight = jnp.ones((scen, tile), f32)
    for step in range(ITERS):
        mix = (step + 1.0) / (step + 2.0)
        last = step == ITERS - 1
        if step:
            parts = butterfly(terms, "rowblk", 2, 2)
            (other_turned,) = call(
                turn_other_kernel,
                [grid, other, terms],
                [SMEM_SPEC] + [VMEM_SPEC] * 2,
                [tiles_like],
                [VMEM_SPEC],
                [],
                turning,
            )
            vectors = [*parts, price, limit, start]
            point, weight, terms = call(
                functools.partial(primal_kernel, mix, True, len(parts)),
                [*own, turned, other_turned, *vectors, grid, weight, primal_norm, point],
                [SMEM_SPEC] * 3 + [VMEM_SPEC] * (2 + len(vectors)) + [SMEM_SPEC] + [VMEM_SPEC] * 3,
                [col_state, small, row_terms],
                [VMEM_SPEC] * 3,
                to_rows,
            )
        else:
            vectors = [*parts, price, limit, start]
            point, terms = call(
                functools.partial(primal_kernel, mix, False, len(parts)),
                [*own, turned, other, *vectors, grid],
                [SMEM_SPEC] * 3 + [VMEM_SPEC] * (2 + len(vectors)) + [SMEM_SPEC],
                [col_state, row_terms],
                [VMEM_SPEC] * 2,
                to_rows,
            )
        parts = butterfly(terms, "colblk", 4)
        if len(parts) == 4:
            parts = [parts[n] for n in (0, 2, 1, 3)]
        if step == 0:
            lines = call(
                row_kernel,
                [extra, demand, row_flag, dual_start, terms],
                [VMEM_SPEC] * 5,
                [row_state] * 3,
                [VMEM_SPEC] * 3,
                [],
            )
        vectors = [*parts, weight, *lines]
        if last:
            keep, send, terms = call(
                functools.partial(dual_kernel, mix, True, len(parts)),
                [*vectors, dual],
                [VMEM_SPEC] * (1 + len(vectors)),
                [row_half, row_half, small],
                [VMEM_SPEC] * 3,
                [],
            )
        else:
            dual, primal_norm, terms = call(
                functools.partial(dual_kernel, mix, False, len(parts)),
                [*own, grid, tiles, other, *vectors],
                [SMEM_SPEC] * 4 + [VMEM_SPEC] * (2 + len(vectors)),
                [row_state, small, col_terms],
                [VMEM_SPEC] * 3,
                to_cols,
            )
    parts = butterfly(terms, "rowblk", 4)
    (both,) = call(
        gather_kernel,
        [point, send],
        [VMEM_SPEC] * 2,
        [pltpu.VMEM((col_quads + row_quads // 2, 2 * scen, tile), f32)],
        [VMEM_SPEC],
        [],
    )
    halves = [point, keep, swap(both, "rowblk", 1)]
    shapes = [primal_start.shape, dual_start.shape]
    point, dual = call(
        result_kernel,
        halves,
        [VMEM_SPEC] * 3,
        [jax.ShapeDtypeStruct(shape, f32) for shape in shapes],
        [FAR_SPEC] * 2,
        [pltpu.VMEM(shape, f32) for shape in shapes] + [pltpu.SemaphoreType.DMA((2,))],
    )
    (weight,) = call(
        functools.partial(weight_kernel, 2.0 / lax.axis_size("rowblk")),
        [*parts, far(dual)],
        [VMEM_SPEC] * len(parts) + [FAR_SPEC],
        [jax.ShapeDtypeStruct((1, scen), f32)],
        [VMEM_SPEC],
        [],
    )
    return point, dual, weight.reshape(scen)


def solution(mesh):
    return jax.shard_map(
        on_device,
        mesh=mesh,
        in_specs=(
            P(("groups", "rowblk", "colblk"), None, None),
            P(("groups", "rowblk", "colblk")),
            P(("groups", "rowblk", "colblk")),
            P(("groups", "rowblk", "colblk")),
            P(("groups", "colblk")),
            P(None, ("groups", "rowblk")),
            P(("groups", "colblk")),
            P(("groups", "colblk")),
            P(("groups", "rowblk")),
            P(None, ("groups", "colblk")),
            P(None, ("groups", "rowblk")),
        ),
        out_specs=(P(None, ("groups", "colblk")), P(None, ("groups", "rowblk")), P("groups")),
        check_vma=False,
    )
```

```python
import functools

import jax
import jax.numpy as jnp
from jax import lax
from jax.experimental import pallas as pl
from jax.experimental.pallas import tpu as pltpu
from jax.sharding import PartitionSpec as P

ITERS = 2
ETA = 0.3
EPS = 1e-06
PART = 24
HALF_PARTS = (32, 16, 24)
VMEM_LIMIT = 8 * 1024 * 1024

SMEM_SPEC = pl.BlockSpec(memory_space=pltpu.SMEM)
VMEM_SPEC = pl.BlockSpec(memory_space=pltpu.VMEM)
FAR_SPEC = pl.BlockSpec(memory_space=pltpu.HBM)


def top(shape):
    return lax.broadcasted_iota(jnp.int32, shape, 0) < shape[0] // 2


def turn_rows(value):
    return pltpu.roll(value, value.shape[0] // 2, 0)


def upper_half(a, b):
    return jnp.where(top(a.shape), a, turn_rows(b))


def lower_half(a, b):
    return jnp.where(top(a.shape), turn_rows(a), b)


def mine_first(value, odd):
    return jnp.where(odd, turn_rows(value), value)


def split_rows(value):
    high = value.astype(jnp.bfloat16)
    low = (value - high.astype(jnp.float32)).astype(jnp.bfloat16)
    return jnp.concatenate([high, low], axis=0)


def add_up(terms):
    while len(terms) > 1:
        terms = [terms[i] + terms[i + 1] for i in range(0, len(terms), 2)]
    return terms[0]


def over_parts(tiles, live, part, sizes=(PART,)):
    total, first, n = tiles.shape[0], 0, 0
    while first < total:
        size = min(sizes[min(n, len(sizes) - 1)], total - first)
        pl.when(first < live)(functools.partial(part, first, size))
        first, n = first + size, n + 1


def first_products(count, rows, cols, tiles, source, acc, ready):
    spare, scen = acc.shape[0] - 1, acc.shape[1]
    live = count[0]
    acc[...] = jnp.zeros_like(acc)

    def part(first, size):
        ready(first)
        landing, results = [], []
        for g in range(first, first + size):
            landing.append(jnp.where(g < live, cols[g], spare))
        pair = 2 if size % 2 == 0 else 1
        for g in range(first, first + size, pair):
            picked = [source[rows[g + k]] for k in range(pair)]
            if pair == 2:
                blank = jnp.zeros_like(picked[0])
                left = jnp.concatenate(
                    [
                        jnp.concatenate([picked[0], blank], axis=1),
                        jnp.concatenate([blank, picked[1]], axis=1),
                    ],
                    axis=0,
                )
                right = jnp.concatenate([tiles[g], tiles[g + 1]], axis=0)
            else:
                left, right = picked[0], tiles[g]
            product = jnp.dot(left, right, preferred_element_type=jnp.float32)
            for k in range(pair):
                own = product[2 * scen * k : 2 * scen * (k + 1)]
                results.append(own[:scen] + own[scen:])
        for where, value in zip(landing, results):
            acc[where] += value

    over_parts(tiles, live, part)


def half_products(live, reads, lands, tiles, depth, source, acc):
    spare = acc.shape[0] - 1
    dims = (((1,), (depth,)), ((), ()))

    def part(first, size):
        landing, results = [], []
        for g in range(first, first + size):
            landing.append(jnp.where(g < live, lands(g), spare))
        pair = 2 if size % 2 == 0 else 1
        for g in range(first, first + size, pair):
            left = jnp.concatenate([source[k, reads(g + k)] for k in range(pair)], axis=1)
            right = jnp.concatenate([tiles[g + k] for k in range(pair)], axis=depth)
            product = lax.dot_general(left, right, dims, preferred_element_type=jnp.float32)
            rows = product.shape[0] // 2
            results += [product[rows * k : rows * (k + 1)] for k in range(pair)]
        for where, value in zip(landing, results):
            acc[where] += value

    over_parts(tiles, live, part, HALF_PARTS)


def put_source(source, k, quad):
    q, rows = source.shape[1] // 4, quad.shape[0] // 2
    high = quad.astype(jnp.bfloat16).astype(jnp.float32)
    low = quad - high
    for h in range(2):
        a, b = high[rows * h : rows * (h + 1)], low[rows * h : rows * (h + 1)]
        for j, block in ((0, upper_half(a, b)), (1, lower_half(a, b))):
            blank = jnp.zeros_like(block)
            where = k + (2 * h + j) * q
            source[0, where] = jnp.concatenate([block, blank], axis=0).astype(jnp.bfloat16)
            source[1, where] = jnp.concatenate([blank, block], axis=0).astype(jnp.bfloat16)


def pack(acc, out, norm, slot):
    q = (acc.shape[0] - 1) // 4
    for k in range(q):
        sums = [acc[k + j * q] for j in range(4)]
        sums = [value + turn_rows(value) for value in sums]
        halves = [jnp.where(top(sums[0].shape), sums[2 * h], sums[2 * h + 1]) for h in range(2)]
        out[k] = jnp.concatenate(halves, axis=0).astype(jnp.bfloat16)
    lanes = lax.broadcasted_iota(jnp.int32, acc.shape[1:], 1)
    out[q] = split_rows(jnp.where(lanes == slot, norm, 0.0))


def total_norm(parts):
    both = add_up([p[p.shape[0] - 1].astype(jnp.float32) for p in parts])
    rows = both.shape[0] // 2
    return jnp.sum(both[:rows] + both[rows:], axis=1, keepdims=True)


def partial_norm(squares):
    rows = squares.shape[0] // 2
    both = squares[:rows] + squares[rows:]
    return jnp.sum(both + turn_rows(both), axis=1, keepdims=True)


def quad_of_rows(array, k):
    q = array.shape[0] // 4
    rows = [array[k + j * q : k + j * q + 1, :] for j in range(4)]
    shape = (8, array.shape[1])
    return jnp.concatenate([jnp.where(top(shape), rows[2 * h], rows[2 * h + 1]) for h in range(2)], axis=0)


def pair_of_blocks(array, k, gap, odd):
    tile = 128
    a, b = (mine_first(array[:, n * tile : (n + 1) * tile], odd) for n in (k, k + gap))
    return upper_half(a, b), lower_half(a, b)


def is_odd():
    return lax.rem(lax.axis_index("rowblk"), 2) == 1


def grid_lines(count, rows, cols, shape):
    lanes, lines = (lax.broadcasted_iota(jnp.int32, (shape[0] // 2, shape[1]), n) for n in (1, 0))
    ways = 4
    found = []
    for index in (rows, cols):
        terms = [jnp.zeros(lanes.shape, jnp.int32)] * ways
        for g in range(index.shape[0]):
            terms[g % ways] = jnp.where(lanes == g, index[g], terms[g % ways])
        found.append(add_up(terms))
    both = jnp.where(lines == 0, found[0], jnp.where(lines == 1, found[1], count[0]))
    both = both.astype(jnp.float32)
    return jnp.concatenate([both, jnp.zeros_like(both)], axis=0).astype(jnp.bfloat16)


def first_kernel(*refs):
    count, rows_far, cols_far, tiles_far, dual_far, keep, send, tiles, rows, cols, source, acc, dual, sems = refs
    tile = tiles.shape[1]
    get_dual = pltpu.make_async_copy(dual_far, dual, sems.at[2])
    get_dual.start()
    copies = [
        pltpu.make_async_copy(rows_far, rows, sems.at[0]),
        pltpu.make_async_copy(cols_far, cols, sems.at[1]),
    ]
    for copy in copies:
        copy.start()
    get_tiles = {}
    for n, first in enumerate(range(0, tiles.shape[0], PART)):
        span = pl.ds(first, min(PART, tiles.shape[0] - first))
        get_tiles[first] = pltpu.make_async_copy(tiles_far.at[span], tiles.at[span], sems.at[3 + n])
        pl.when(first < count[0])(get_tiles[first].start)
    get_dual.wait()
    for b in range(source.shape[0]):
        source[b] = split_rows(dual[:, b * tile : (b + 1) * tile])
    for copy in copies:
        copy.wait()
    lines = grid_lines(count, rows, cols, send.shape[1:])
    first_products(count, rows, cols, tiles, source, acc, lambda first: get_tiles[first].wait())
    odd = is_odd()
    q = keep.shape[0]
    for k in range(q):
        halves = []
        for h in range(2):
            a, b = (mine_first(acc[k + (2 * h + j) * q], odd) for j in range(2))
            halves.append((upper_half(a, b), lower_half(a, b)))
        keep[k] = jnp.concatenate([halves[0][0], halves[1][0]], axis=0)
        send[k] = jnp.concatenate([halves[0][1], halves[1][1]], axis=0).astype(jnp.bfloat16)
    send[q] = lines


def turn_tiles(live, tiles, turned):
    def part(first, size):
        for g in range(first, first + size):
            turned[g] = tiles[g].T

    over_parts(tiles, live, part)


def turn_kernel(count, tiles, after, turned):
    del after
    turn_tiles(count[0], tiles, turned)


def extra_kernel(dual, demand, flag, after, extra):
    del after
    half = flag.shape[0] // 2
    odd = is_odd()
    for k in range(half):
        extra[k] = pair_of_blocks(dual, k, half, odd)[1]
        extra[half + k] = pair_of_blocks(demand, k, half, odd)[1]
    for n in range(flag.shape[0] // 8):
        extra[2 * half + n] = flag[8 * n : 8 * (n + 1), :].astype(jnp.float32)


def grid_kernel(received, after, grid, whole, sem):
    del after
    last = received[received.shape[0] - 1].astype(jnp.float32)
    whole[...] = last[: whole.shape[0]].astype(jnp.int32)
    copy = pltpu.make_async_copy(whole, grid, sem)
    copy.start()
    copy.wait()


def col_kernel(begin, cost, upper, flag, after, start, price, limit):
    del after
    odd = is_odd()
    q = start.shape[0]
    for k in range(q):
        start[k] = jnp.concatenate([pair_of_blocks(begin, k + 2 * h * q, q, odd)[0] for h in range(2)], axis=0)
        price[k] = quad_of_rows(cost, k)
        limit[k] = jnp.where(quad_of_rows(flag, k) > 0, quad_of_rows(upper, k), jnp.inf)


def row_kernel(extra, demand, flag, begin, after, start, right, floor):
    del after
    odd = is_odd()
    half, tile = start.shape[0], start.shape[2]
    for k in range(half):
        start[k] = jnp.concatenate([pair_of_blocks(begin, k, half, odd)[0], extra[k]], axis=0)
        right[k] = jnp.concatenate([pair_of_blocks(demand, k, half, odd)[0], extra[half + k]], axis=0)
        own = [flag[n : n + 1, :].astype(jnp.float32) for n in (k, k + half)]
        far = [extra[2 * half + n // 8, n % 8 : n % 8 + 1, :] for n in (k, k + half)]
        marks = [jnp.where(top((8, tile)), a, b) for a, b in (own, far)]
        floor[k] = jnp.where(jnp.concatenate(marks, axis=0) > 0.0, 0.0, -jnp.inf)


def turn_other_kernel(grid, tiles, after, turned):
    del after
    turn_tiles(grid[2, 0], tiles, turned)


def primal_kernel(mix, last, n_parts, *refs):
    count, rows, cols, tiles = refs[:4]
    parts = refs[4 : 4 + n_parts]
    price, limit, start, *refs = refs[4 + n_parts :]
    if last:
        other, grid, weight_in, primal_norm, point, point_out, weight_out, out, source, acc = refs
        dual_norm = total_norm(parts)
        weight = weight_in[:, :1]
        ratio = (dual_norm + EPS) / (primal_norm[:, :1] + EPS)
        weight = jnp.sqrt(weight * jnp.sqrt(ratio))
        weight_out[...] = jnp.broadcast_to(weight, weight_out.shape)
    else:
        point_out, source, acc, norm_out = refs
        point = start
        weight = jnp.ones((8, 1), jnp.float32)
    q = point_out.shape[0]
    tile = point_out.shape[2]
    tau = jnp.broadcast_to(ETA / weight, (weight.shape[0], tile))
    tau = jnp.concatenate([tau, tau], axis=0)
    squares = jnp.zeros_like(tau)
    for k in range(q):
        value = add_up([p[k].astype(jnp.float32) for p in parts])
        old = point[k]
        moved = old - tau * (price[k] - value)
        x_hat = jnp.maximum(jnp.minimum(moved, limit[k]), 0.0)
        step = x_hat - old
        squares += step * step
        x_bar = 2.0 * x_hat - old
        point_out[k] = mix * x_bar + (1.0 - mix) * start[k]
        put_source(source, k, x_bar)
    acc[...] = jnp.zeros_like(acc)
    near = (acc.shape[0] - 1) // 2
    half_products(count[0], lambda g: cols[g], lambda g: rows[g], tiles, 0, source, acc)
    norm = partial_norm(squares)
    if last:
        half_products(grid[2, 0], lambda g: grid[1, g], lambda g: near + grid[0, g], other, 0, source, acc)
        pack(acc, out, norm, lax.axis_index("colblk"))
    else:
        norm_out[...] = jnp.broadcast_to(norm, norm_out.shape)


def other_kernel(grid, other, source, own, norm, out, acc):
    acc[...] = own[...]
    near = (acc.shape[0] - 1) // 2
    half_products(grid[2, 0], lambda g: grid[1, g], lambda g: near + grid[0, g], other, 1, source, acc)
    pack(acc, out, norm[:, :1], lax.axis_index("colblk"))


def dual_kernel(mix, last, n_parts, *refs):
    if last:
        parts = refs[:n_parts]
        refs = refs[n_parts:]
        weight, start, right, floor, dual, keep, send, small = refs
    else:
        count, rows, cols, grid, tiles, other = refs[:6]
        parts = refs[6 : 6 + n_parts]
        refs = refs[6 + n_parts :]
        weight, start, right, floor, dual_out, primal_norm, out, source, acc = refs
        dual = start
    if n_parts == 4:
        parts = [parts[0], parts[2], parts[1], parts[3]]
    primal_total = total_norm(parts)
    sigma = jnp.concatenate([ETA * weight[...]] * 2, axis=0)
    squares = jnp.zeros_like(sigma)
    for k in range(start.shape[0]):
        value = add_up([p[k].astype(jnp.float32) for p in parts])
        old = dual[k]
        moved = old + sigma * (right[k] - value)
        y_hat = jnp.maximum(moved, floor[k])
        step = y_hat - old
        squares += step * step
        new = mix * (2.0 * y_hat - old) + (1.0 - mix) * start[k]
        if last:
            keep[k] = new[:8]
            send[k] = new[8:]
        else:
            dual_out[k] = new
            put_source(source, k, new)
    dual_norm = partial_norm(squares)
    if last:
        lanes = lax.broadcasted_iota(jnp.int32, small.shape, 1)
        first = jnp.where(is_odd(), 3, 0)
        values = jnp.where(lanes == first, dual_norm, 0.0)
        values = jnp.where(lanes == first + 1, primal_total, values)
        small[...] = jnp.where(lanes == first + 2, weight[...], values)
    else:
        primal_norm[...] = jnp.broadcast_to(primal_total, primal_norm.shape)
        acc[...] = jnp.zeros_like(acc)
        near = source.shape[1] // 2
        half_products(count[0], lambda g: rows[g], lambda g: cols[g], tiles, 0, source, acc)
        half_products(grid[2, 0], lambda g: near + grid[0, g], lambda g: grid[1, g], other, 0, source, acc)
        pack(acc, out, dual_norm, lax.axis_index("rowblk"))


def join(mine, others, out):
    tile = mine.shape[2]
    odd = is_odd()
    q, pairs = mine.shape[0], mine.shape[1] // 8
    for k in range(q):
        for h in range(pairs):
            a, b = mine[k, 8 * h : 8 * (h + 1), :], others(k, h)
            a, b = jnp.where(odd, b, a), jnp.where(odd, a, b)
            for j, value in ((0, upper_half(a, b)), (1, lower_half(a, b))):
                n = k + (2 * h + j) * q
                out[:, n * tile : (n + 1) * tile] = value


def gather_kernel(point, send, both):
    q = point.shape[0]
    both[:q] = point[...]
    for k in range(send.shape[0] // 2):
        both[q + k] = jnp.concatenate([send[2 * k], send[2 * k + 1]], axis=0)


def result_kernel(mine_x, mine_y, other, far_x, far_y, x_out, y_out, sems):
    copies = []
    q = mine_x.shape[0]
    from_x = lambda k, h: other[k, 8 * h : 8 * (h + 1), :]
    from_y = lambda k, h: other[q + k // 2, 8 * (k % 2) : 8 * (k % 2 + 1), :]
    for n, (mine, others, out, target) in enumerate(((mine_x, from_x, x_out, far_x), (mine_y, from_y, y_out, far_y))):
        join(mine, others, out)
        copies.append(pltpu.make_async_copy(out, target, sems.at[n]))
        copies[-1].start()
    for copy in copies:
        copy.wait()


def weight_kernel(share, *refs):
    *parts, after, out = refs
    del after
    both = add_up([p[...] for p in parts])
    found = []
    for first in (0, 3):
        dual_norm, primal_norm, weight = (both[:, first + n : first + n + 1] for n in range(3))
        ratio = (dual_norm + EPS) / (primal_norm * share + EPS)
        found.append(jnp.sqrt(weight * share * jnp.sqrt(ratio)))
    weight = jnp.where(top(found[0].shape), found[0], found[1])
    lanes, rows = (lax.broadcasted_iota(jnp.int32, both.shape, n) for n in (1, 0))
    row = jnp.sum(jnp.where(lanes == rows, weight, 0.0), axis=0, keepdims=True)
    out[...] = row[:, : out.shape[1]]


def call(kernel, inputs, in_specs, outputs, out_specs, scratch, cost=None):
    return pl.pallas_call(
        kernel,
        out_shape=outputs,
        in_specs=in_specs,
        out_specs=out_specs,
        scratch_shapes=scratch,
        cost_estimate=cost,
        compiler_params=pltpu.CompilerParams(vmem_limit_bytes=VMEM_LIMIT),
    )(*inputs)


def far(value):
    return pltpu.with_memory_space_constraint(value, pltpu.HBM)


def swap(value, axis, mask):
    size = lax.axis_size(axis)
    return lax.ppermute(value, axis, [(i, i ^ mask) for i in range(size)])


def butterfly(value, axis, radix, mask=1):
    size = lax.axis_size(axis)
    parts = [value]
    while mask < size:
        total = add_up([p.astype(jnp.float32) for p in parts]).astype(value.dtype)
        span = min(radix, size // mask)
        parts = [total] + [swap(total, axis, mask * k) for k in range(1, span)]
        mask *= span
    return parts


def on_device(
    tiles,
    tile_row,
    tile_col,
    tile_count,
    cost,
    demand,
    upper,
    col_flag,
    row_flag,
    primal_start,
    dual_start,
):
    tile = tiles.shape[1]
    total = tile_row.shape[0]
    scen = primal_start.shape[0]
    col_blocks = primal_start.shape[1] // tile
    row_blocks = dual_start.shape[1] // tile
    bf16, f32, i32 = jnp.bfloat16, jnp.float32, jnp.int32
    cost, upper, col_flag = (v.reshape(col_blocks, tile) for v in (cost, upper, col_flag))
    row_flag = row_flag.reshape(row_blocks, tile)

    small = pltpu.VMEM((scen, tile), f32)
    col_quads, row_quads = col_blocks // 4, row_blocks // 2
    col_state = pltpu.VMEM((col_quads, 2 * scen, tile), f32)
    row_state = pltpu.VMEM((row_quads, 2 * scen, tile), f32)
    row_half = pltpu.VMEM((row_quads, scen, tile), f32)
    col_terms = pltpu.VMEM((col_quads + 1, 2 * scen, tile), bf16)
    row_terms = pltpu.VMEM((row_quads + 1, 2 * scen, tile), bf16)
    tiles_like = pltpu.VMEM(tiles.shape, tiles.dtype)
    index = pltpu.SMEM((total,), i32)
    to_cols = [
        pltpu.VMEM((2, 2 * row_blocks, 2 * scen, tile), bf16),
        pltpu.VMEM((col_blocks + 1, scen, tile), f32),
    ]
    to_rows = [
        pltpu.VMEM((2, col_blocks, 2 * scen, tile), bf16),
        pltpu.VMEM((2 * row_blocks + 1, scen, tile), f32),
    ]
    turning = pl.CostEstimate(flops=0, bytes_accessed=2 * tiles.size * 2, transcendentals=0)

    keep, send, tiles, rows, cols = call(
        first_kernel,
        [tile_count, far(tile_row), far(tile_col), far(tiles), far(dual_start)],
        [SMEM_SPEC] + [FAR_SPEC] * 4,
        [col_state, col_terms, tiles_like, index, index],
        [VMEM_SPEC] * 3 + [SMEM_SPEC] * 2,
        [
            pltpu.VMEM((row_blocks, 2 * scen, tile), bf16),
            pltpu.VMEM((col_blocks + 1, scen, tile), f32),
            pltpu.VMEM(dual_start.shape, f32),
            pltpu.SemaphoreType.DMA((3 + pl.cdiv(total, PART),)),
        ],
    )
    received = swap(send, "rowblk", 1)
    terms = (keep + received[:col_quads].astype(f32)).astype(bf16)
    held_tiles, terms = lax.optimization_barrier((tiles, terms))
    parts = butterfly(terms, "rowblk", 2, 2)
    other = swap(held_tiles, "rowblk", 1)
    (turned,) = call(
        turn_kernel,
        [tile_count, tiles, terms],
        [SMEM_SPEC] + [VMEM_SPEC] * 2,
        [tiles_like],
        [VMEM_SPEC],
        [],
        turning,
    )
    (extra,) = call(
        extra_kernel,
        [dual_start, demand, row_flag, terms],
        [VMEM_SPEC] * 4,
        [pltpu.VMEM((2 * row_quads + row_blocks // 8, scen, tile), f32)],
        [VMEM_SPEC],
        [],
    )
    extra = swap(extra, "rowblk", 1)
    columns = call(
        col_kernel,
        [primal_start, cost, upper, col_flag, terms],
        [VMEM_SPEC] * 5,
        [col_state] * 3,
        [VMEM_SPEC] * 3,
        [],
    )
    start, price, limit = columns
    (grid,) = call(
        grid_kernel,
        [received, terms],
        [VMEM_SPEC] * 2,
        [pltpu.SMEM((scen, tile), i32)],
        [SMEM_SPEC],
        [pltpu.VMEM((scen, tile), i32), pltpu.SemaphoreType.DMA],
    )
    own = [tile_count, rows, cols]
    weight = jnp.ones((scen, tile), f32)
    for step in range(ITERS):
        mix = (step + 1.0) / (step + 2.0)
        last = step == ITERS - 1
        if step:
            parts = butterfly(terms, "rowblk", 2, 2)
            (other_turned,) = call(
                turn_other_kernel,
                [grid, other, terms],
                [SMEM_SPEC] + [VMEM_SPEC] * 2,
                [tiles_like],
                [VMEM_SPEC],
                [],
                turning,
            )
            vectors = [*parts, price, limit, start]
            point, weight, terms = call(
                functools.partial(primal_kernel, mix, True, len(parts)),
                [*own, turned, *vectors, other_turned, grid, weight, primal_norm, point],
                [SMEM_SPEC] * 3 + [VMEM_SPEC] * (2 + len(vectors)) + [SMEM_SPEC] + [VMEM_SPEC] * 3,
                [col_state, small, row_terms],
                [VMEM_SPEC] * 3,
                to_rows,
            )
        else:
            vectors = [*parts, price, limit, start]
            point, *half_way = call(
                functools.partial(primal_kernel, mix, False, len(parts)),
                [*own, turned, *vectors],
                [SMEM_SPEC] * 3 + [VMEM_SPEC] * (1 + len(vectors)),
                [col_state, *to_rows, small],
                [VMEM_SPEC] * 4,
                [],
            )
            (terms,) = call(
                other_kernel,
                [grid, other, *half_way],
                [SMEM_SPEC] + [VMEM_SPEC] * 4,
                [row_terms],
                [VMEM_SPEC],
                [to_rows[1]],
            )
        parts = butterfly(terms, "colblk", 4)
        if len(parts) == 4:
            parts = [parts[n] for n in (0, 2, 1, 3)]
        if step == 0:
            lines = call(
                row_kernel,
                [extra, demand, row_flag, dual_start, terms],
                [VMEM_SPEC] * 5,
                [row_state] * 3,
                [VMEM_SPEC] * 3,
                [],
            )
        vectors = [*parts, weight, *lines]
        if last:
            keep, send, terms = call(
                functools.partial(dual_kernel, mix, True, len(parts)),
                [*vectors, dual],
                [VMEM_SPEC] * (1 + len(vectors)),
                [row_half, row_half, small],
                [VMEM_SPEC] * 3,
                [],
            )
        else:
            dual, primal_norm, terms = call(
                functools.partial(dual_kernel, mix, False, len(parts)),
                [*own, grid, tiles, other, *vectors],
                [SMEM_SPEC] * 4 + [VMEM_SPEC] * (2 + len(vectors)),
                [row_state, small, col_terms],
                [VMEM_SPEC] * 3,
                to_cols,
            )
    parts = butterfly(terms, "rowblk", 4)
    (both,) = call(
        gather_kernel,
        [point, send],
        [VMEM_SPEC] * 2,
        [pltpu.VMEM((col_quads + row_quads // 2, 2 * scen, tile), f32)],
        [VMEM_SPEC],
        [],
    )
    halves = [point, keep, swap(both, "rowblk", 1)]
    shapes = [primal_start.shape, dual_start.shape]
    point, dual = call(
        result_kernel,
        halves,
        [VMEM_SPEC] * 3,
        [jax.ShapeDtypeStruct(shape, f32) for shape in shapes],
        [FAR_SPEC] * 2,
        [pltpu.VMEM(shape, f32) for shape in shapes] + [pltpu.SemaphoreType.DMA((2,))],
    )
    (weight,) = call(
        functools.partial(weight_kernel, 2.0 / lax.axis_size("rowblk")),
        [*parts, far(dual)],
        [VMEM_SPEC] * len(parts) + [FAR_SPEC],
        [jax.ShapeDtypeStruct((1, scen), f32)],
        [VMEM_SPEC],
        [],
    )
    return point, dual, weight.reshape(scen)


def solution(mesh):
    return jax.shard_map(
        on_device,
        mesh=mesh,
        in_specs=(
            P(("groups", "rowblk", "colblk"), None, None),
            P(("groups", "rowblk", "colblk")),
            P(("groups", "rowblk", "colblk")),
            P(("groups", "rowblk", "colblk")),
            P(("groups", "colblk")),
            P(None, ("groups", "rowblk")),
            P(("groups", "colblk")),
            P(("groups", "colblk")),
            P(("groups", "rowblk")),
            P(None, ("groups", "colblk")),
            P(None, ("groups", "rowblk")),
        ),
        out_specs=(P(None, ("groups", "colblk")), P(None, ("groups", "rowblk")), P("groups")),
        check_vma=False,
    )
```

```python
import functools

import jax
import jax.numpy as jnp
from jax import lax
from jax.experimental import pallas as pl
from jax.experimental.pallas import tpu as pltpu
from jax.sharding import PartitionSpec as P

ITERS = 2
ETA = 0.3
EPS = 1e-06
PART = 24
HALF_PARTS = (48, 24)
VMEM_LIMIT = 8 * 1024 * 1024

SMEM_SPEC = pl.BlockSpec(memory_space=pltpu.SMEM)
VMEM_SPEC = pl.BlockSpec(memory_space=pltpu.VMEM)
FAR_SPEC = pl.BlockSpec(memory_space=pltpu.HBM)


def top(shape):
    return lax.broadcasted_iota(jnp.int32, shape, 0) < shape[0] // 2


def turn_rows(value):
    return pltpu.roll(value, value.shape[0] // 2, 0)


def upper_half(a, b):
    return jnp.where(top(a.shape), a, turn_rows(b))


def lower_half(a, b):
    return jnp.where(top(a.shape), turn_rows(a), b)


def mine_first(value, odd):
    return jnp.where(odd, turn_rows(value), value)


def split_rows(value):
    high = value.astype(jnp.bfloat16)
    low = (value - high.astype(jnp.float32)).astype(jnp.bfloat16)
    return jnp.concatenate([high, low], axis=0)


def add_up(terms):
    while len(terms) > 1:
        terms = [terms[i] + terms[i + 1] for i in range(0, len(terms), 2)]
    return terms[0]


def over_parts(tiles, live, part, sizes=(PART,)):
    total, first, n = tiles.shape[0], 0, 0
    while first < total:
        size = min(sizes[min(n, len(sizes) - 1)], total - first)
        pl.when(first < live)(functools.partial(part, first, size))
        first, n = first + size, n + 1


def first_products(count, rows, cols, tiles, source, acc, ready):
    spare, scen = acc.shape[0] - 1, acc.shape[1]
    live = count[0]
    acc[...] = jnp.zeros_like(acc)

    def part(first, size):
        ready(first)
        landing, results = [], []
        for g in range(first, first + size):
            landing.append(jnp.where(g < live, cols[g], spare))
        pair = 2 if size % 2 == 0 else 1
        for g in range(first, first + size, pair):
            picked = [source[rows[g + k]] for k in range(pair)]
            if pair == 2:
                blank = jnp.zeros_like(picked[0])
                left = jnp.concatenate(
                    [
                        jnp.concatenate([picked[0], blank], axis=1),
                        jnp.concatenate([blank, picked[1]], axis=1),
                    ],
                    axis=0,
                )
                right = jnp.concatenate([tiles[g], tiles[g + 1]], axis=0)
            else:
                left, right = picked[0], tiles[g]
            product = jnp.dot(left, right, preferred_element_type=jnp.float32)
            for k in range(pair):
                own = product[2 * scen * k : 2 * scen * (k + 1)]
                results.append(own[:scen] + own[scen:])
        for where, value in zip(landing, results):
            acc[where] += value

    over_parts(tiles, live, part)


def half_products(live, reads, lands, tiles, depth, source, acc):
    spare = acc.shape[0] - 1
    dims = (((1,), (depth,)), ((), ()))

    def part(first, size):
        landing, results = [], []
        for g in range(first, first + size):
            landing.append(jnp.where(g < live, lands(g), spare))
        pair = 2 if size % 2 == 0 else 1
        for g in range(first, first + size, pair):
            left = jnp.concatenate([source[k, reads(g + k)] for k in range(pair)], axis=1)
            right = jnp.concatenate([tiles[g + k] for k in range(pair)], axis=depth)
            product = lax.dot_general(left, right, dims, preferred_element_type=jnp.float32)
            rows = product.shape[0] // 2
            results += [product[rows * k : rows * (k + 1)] for k in range(pair)]
        for where, value in zip(landing, results):
            acc[where] += value

    over_parts(tiles, live, part, HALF_PARTS)


def put_source(source, k, quad):
    q, rows = source.shape[1] // 4, quad.shape[0] // 2
    high = quad.astype(jnp.bfloat16).astype(jnp.float32)
    low = quad - high
    for h in range(2):
        a, b = high[rows * h : rows * (h + 1)], low[rows * h : rows * (h + 1)]
        for j, block in ((0, upper_half(a, b)), (1, lower_half(a, b))):
            blank = jnp.zeros_like(block)
            where = k + (2 * h + j) * q
            source[0, where] = jnp.concatenate([block, blank], axis=0).astype(jnp.bfloat16)
            source[1, where] = jnp.concatenate([blank, block], axis=0).astype(jnp.bfloat16)


def pack(acc, out, norm, slot):
    q = (acc.shape[0] - 1) // 4
    for k in range(q):
        sums = [acc[k + j * q] for j in range(4)]
        sums = [value + turn_rows(value) for value in sums]
        halves = [jnp.where(top(sums[0].shape), sums[2 * h], sums[2 * h + 1]) for h in range(2)]
        out[k] = jnp.concatenate(halves, axis=0).astype(jnp.bfloat16)
    lanes = lax.broadcasted_iota(jnp.int32, acc.shape[1:], 1)
    out[q] = split_rows(jnp.where(lanes == slot, norm, 0.0))


def total_norm(parts):
    both = add_up([p[p.shape[0] - 1].astype(jnp.float32) for p in parts])
    rows = both.shape[0] // 2
    return jnp.sum(both[:rows] + both[rows:], axis=1, keepdims=True)


def partial_norm(squares):
    rows = squares.shape[0] // 2
    both = squares[:rows] + squares[rows:]
    return jnp.sum(both + turn_rows(both), axis=1, keepdims=True)


def quad_of_rows(array, k):
    q = array.shape[0] // 4
    rows = [array[k + j * q : k + j * q + 1, :] for j in range(4)]
    shape = (8, array.shape[1])
    return jnp.concatenate([jnp.where(top(shape), rows[2 * h], rows[2 * h + 1]) for h in range(2)], axis=0)


def pair_of_blocks(array, k, gap, odd):
    tile = 128
    a, b = (mine_first(array[:, n * tile : (n + 1) * tile], odd) for n in (k, k + gap))
    return upper_half(a, b), lower_half(a, b)


def is_odd():
    return lax.rem(lax.axis_index("rowblk"), 2) == 1


def grid_lines(count, rows, cols, shape):
    lanes, lines = (lax.broadcasted_iota(jnp.int32, (shape[0] // 2, shape[1]), n) for n in (1, 0))
    ways = 4
    found = []
    for index in (rows, cols):
        terms = [jnp.zeros(lanes.shape, jnp.int32)] * ways
        for g in range(index.shape[0]):
            terms[g % ways] = jnp.where(lanes == g, index[g], terms[g % ways])
        found.append(add_up(terms))
    both = jnp.where(lines == 0, found[0], jnp.where(lines == 1, found[1], count[0]))
    both = both.astype(jnp.float32)
    return jnp.concatenate([both, jnp.zeros_like(both)], axis=0).astype(jnp.bfloat16)


def first_kernel(*refs):
    count, rows_far, cols_far, tiles_far, dual_far, keep, send, tiles, rows, cols, source, acc, dual, sems = refs
    tile = tiles.shape[1]
    get_dual = pltpu.make_async_copy(dual_far, dual, sems.at[2])
    get_dual.start()
    copies = [
        pltpu.make_async_copy(rows_far, rows, sems.at[0]),
        pltpu.make_async_copy(cols_far, cols, sems.at[1]),
    ]
    for copy in copies:
        copy.start()
    get_tiles = {}
    for n, first in enumerate(range(0, tiles.shape[0], PART)):
        span = pl.ds(first, min(PART, tiles.shape[0] - first))
        get_tiles[first] = pltpu.make_async_copy(tiles_far.at[span], tiles.at[span], sems.at[3 + n])
        pl.when(first < count[0])(get_tiles[first].start)
    get_dual.wait()
    for b in range(source.shape[0]):
        source[b] = split_rows(dual[:, b * tile : (b + 1) * tile])
    for copy in copies:
        copy.wait()
    lines = grid_lines(count, rows, cols, send.shape[1:])
    first_products(count, rows, cols, tiles, source, acc, lambda first: get_tiles[first].wait())
    odd = is_odd()
    q = keep.shape[0]
    for k in range(q):
        halves = []
        for h in range(2):
            a, b = (mine_first(acc[k + (2 * h + j) * q], odd) for j in range(2))
            halves.append((upper_half(a, b), lower_half(a, b)))
        keep[k] = jnp.concatenate([halves[0][0], halves[1][0]], axis=0)
        send[k] = jnp.concatenate([halves[0][1], halves[1][1]], axis=0).astype(jnp.bfloat16)
    send[q] = lines


def turn_tiles(live, tiles, turned):
    def part(first, size):
        for g in range(first, first + size):
            turned[g] = tiles[g].T

    over_parts(tiles, live, part)


def turn_kernel(count, tiles, after, turned):
    del after
    turn_tiles(count[0], tiles, turned)


def extra_kernel(dual, demand, flag, after, extra):
    del after
    half = flag.shape[0] // 2
    odd = is_odd()
    for k in range(half):
        extra[k] = pair_of_blocks(dual, k, half, odd)[1]
        extra[half + k] = pair_of_blocks(demand, k, half, odd)[1]
    for n in range(flag.shape[0] // 8):
        extra[2 * half + n] = flag[8 * n : 8 * (n + 1), :].astype(jnp.float32)


def grid_kernel(received, after, grid, whole, sem):
    del after
    last = received[received.shape[0] - 1].astype(jnp.float32)
    whole[...] = last[: whole.shape[0]].astype(jnp.int32)
    copy = pltpu.make_async_copy(whole, grid, sem)
    copy.start()
    copy.wait()


def col_kernel(begin, cost, upper, flag, after, start, price, limit):
    del after
    odd = is_odd()
    q = start.shape[0]
    for k in range(q):
        start[k] = jnp.concatenate([pair_of_blocks(begin, k + 2 * h * q, q, odd)[0] for h in range(2)], axis=0)
        price[k] = quad_of_rows(cost, k)
        limit[k] = jnp.where(quad_of_rows(flag, k) > 0, quad_of_rows(upper, k), jnp.inf)


def row_kernel(extra, demand, flag, begin, after, start, right, floor):
    del after
    odd = is_odd()
    half, tile = start.shape[0], start.shape[2]
    for k in range(half):
        start[k] = jnp.concatenate([pair_of_blocks(begin, k, half, odd)[0], extra[k]], axis=0)
        right[k] = jnp.concatenate([pair_of_blocks(demand, k, half, odd)[0], extra[half + k]], axis=0)
        own = [flag[n : n + 1, :].astype(jnp.float32) for n in (k, k + half)]
        far = [extra[2 * half + n // 8, n % 8 : n % 8 + 1, :] for n in (k, k + half)]
        marks = [jnp.where(top((8, tile)), a, b) for a, b in (own, far)]
        floor[k] = jnp.where(jnp.concatenate(marks, axis=0) > 0.0, 0.0, -jnp.inf)


def turn_other_kernel(grid, tiles, after, turned):
    del after
    turn_tiles(grid[2, 0], tiles, turned)


def primal_kernel(mix, last, n_parts, *refs):
    count, rows, cols, tiles = refs[:4]
    parts = refs[4 : 4 + n_parts]
    price, limit, start, *refs = refs[4 + n_parts :]
    if last:
        other, grid, weight_in, primal_norm, point, point_out, weight_out, out, source, acc = refs
        dual_norm = total_norm(parts)
        weight = weight_in[:, :1]
        ratio = (dual_norm + EPS) / (primal_norm[:, :1] + EPS)
        weight = jnp.sqrt(weight * jnp.sqrt(ratio))
        weight_out[...] = jnp.broadcast_to(weight, weight_out.shape)
    else:
        point_out, source, acc, norm_out = refs
        point = start
        weight = jnp.ones((8, 1), jnp.float32)
    q = point_out.shape[0]
    tile = point_out.shape[2]
    tau = jnp.broadcast_to(ETA / weight, (weight.shape[0], tile))
    tau = jnp.concatenate([tau, tau], axis=0)
    squares = jnp.zeros_like(tau)
    for k in range(q):
        value = add_up([p[k].astype(jnp.float32) for p in parts])
        old = point[k]
        moved = old - tau * (price[k] - value)
        x_hat = jnp.maximum(jnp.minimum(moved, limit[k]), 0.0)
        step = x_hat - old
        squares += step * step
        x_bar = 2.0 * x_hat - old
        point_out[k] = mix * x_bar + (1.0 - mix) * start[k]
        put_source(source, k, x_bar)
    acc[...] = jnp.zeros_like(acc)
    near = (acc.shape[0] - 1) // 2
    half_products(count[0], lambda g: cols[g], lambda g: rows[g], tiles, 0, source, acc)
    norm = partial_norm(squares)
    if last:
        half_products(grid[2, 0], lambda g: grid[1, g], lambda g: near + grid[0, g], other, 0, source, acc)
        pack(acc, out, norm, lax.axis_index("colblk"))
    else:
        norm_out[...] = jnp.broadcast_to(norm, norm_out.shape)


def other_kernel(grid, other, source, own, norm, out, acc):
    acc[...] = own[...]
    near = (acc.shape[0] - 1) // 2
    half_products(grid[2, 0], lambda g: grid[1, g], lambda g: near + grid[0, g], other, 1, source, acc)
    pack(acc, out, norm[:, :1], lax.axis_index("colblk"))


def dual_kernel(mix, last, n_parts, *refs):
    if last:
        parts = refs[:n_parts]
        refs = refs[n_parts:]
        weight, start, right, floor, dual, keep, send, small = refs
    else:
        count, rows, cols, grid, tiles, other = refs[:6]
        parts = refs[6 : 6 + n_parts]
        refs = refs[6 + n_parts :]
        weight, start, right, floor, dual_out, primal_norm, out, source, acc = refs
        dual = start
    if n_parts == 4:
        parts = [parts[0], parts[2], parts[1], parts[3]]
    primal_total = total_norm(parts)
    sigma = jnp.concatenate([ETA * weight[...]] * 2, axis=0)
    squares = jnp.zeros_like(sigma)
    for k in range(start.shape[0]):
        value = add_up([p[k].astype(jnp.float32) for p in parts])
        old = dual[k]
        moved = old + sigma * (right[k] - value)
        y_hat = jnp.maximum(moved, floor[k])
        step = y_hat - old
        squares += step * step
        new = mix * (2.0 * y_hat - old) + (1.0 - mix) * start[k]
        if last:
            keep[k] = new[:8]
            send[k] = new[8:]
        else:
            dual_out[k] = new
            put_source(source, k, new)
    dual_norm = partial_norm(squares)
    if last:
        lanes = lax.broadcasted_iota(jnp.int32, small.shape, 1)
        first = jnp.where(is_odd(), 3, 0)
        values = jnp.where(lanes == first, dual_norm, 0.0)
        values = jnp.where(lanes == first + 1, primal_total, values)
        small[...] = jnp.where(lanes == first + 2, weight[...], values)
    else:
        primal_norm[...] = jnp.broadcast_to(primal_total, primal_norm.shape)
        acc[...] = jnp.zeros_like(acc)
        near = source.shape[1] // 2
        half_products(count[0], lambda g: rows[g], lambda g: cols[g], tiles, 0, source, acc)
        half_products(grid[2, 0], lambda g: near + grid[0, g], lambda g: grid[1, g], other, 0, source, acc)
        pack(acc, out, dual_norm, lax.axis_index("rowblk"))


def join(mine, others, out):
    tile = mine.shape[2]
    odd = is_odd()
    q, pairs = mine.shape[0], mine.shape[1] // 8
    for k in range(q):
        for h in range(pairs):
            a, b = mine[k, 8 * h : 8 * (h + 1), :], others(k, h)
            a, b = jnp.where(odd, b, a), jnp.where(odd, a, b)
            for j, value in ((0, upper_half(a, b)), (1, lower_half(a, b))):
                n = k + (2 * h + j) * q
                out[:, n * tile : (n + 1) * tile] = value


def gather_kernel(point, send, both):
    q = point.shape[0]
    both[:q] = point[...]
    for k in range(send.shape[0] // 2):
        both[q + k] = jnp.concatenate([send[2 * k], send[2 * k + 1]], axis=0)


def result_kernel(mine_x, mine_y, other, far_x, far_y, x_out, y_out, sems):
    copies = []
    q = mine_x.shape[0]
    from_x = lambda k, h: other[k, 8 * h : 8 * (h + 1), :]
    from_y = lambda k, h: other[q + k // 2, 8 * (k % 2) : 8 * (k % 2 + 1), :]
    for n, (mine, others, out, target) in enumerate(((mine_x, from_x, x_out, far_x), (mine_y, from_y, y_out, far_y))):
        join(mine, others, out)
        copies.append(pltpu.make_async_copy(out, target, sems.at[n]))
        copies[-1].start()
    for copy in copies:
        copy.wait()


def weight_kernel(share, *refs):
    *parts, after, out = refs
    del after
    both = add_up([p[...] for p in parts])
    found = []
    for first in (0, 3):
        dual_norm, primal_norm, weight = (both[:, first + n : first + n + 1] for n in range(3))
        ratio = (dual_norm + EPS) / (primal_norm * share + EPS)
        found.append(jnp.sqrt(weight * share * jnp.sqrt(ratio)))
    weight = jnp.where(top(found[0].shape), found[0], found[1])
    lanes, rows = (lax.broadcasted_iota(jnp.int32, both.shape, n) for n in (1, 0))
    row = jnp.sum(jnp.where(lanes == rows, weight, 0.0), axis=0, keepdims=True)
    out[...] = row[:, : out.shape[1]]


def call(kernel, inputs, in_specs, outputs, out_specs, scratch, cost=None):
    return pl.pallas_call(
        kernel,
        out_shape=outputs,
        in_specs=in_specs,
        out_specs=out_specs,
        scratch_shapes=scratch,
        cost_estimate=cost,
        compiler_params=pltpu.CompilerParams(vmem_limit_bytes=VMEM_LIMIT),
    )(*inputs)


def far(value):
    return pltpu.with_memory_space_constraint(value, pltpu.HBM)


def swap(value, axis, mask):
    size = lax.axis_size(axis)
    return lax.ppermute(value, axis, [(i, i ^ mask) for i in range(size)])


def butterfly(value, axis, radix, mask=1):
    size = lax.axis_size(axis)
    parts = [value]
    while mask < size:
        total = add_up([p.astype(jnp.float32) for p in parts]).astype(value.dtype)
        span = min(radix, size // mask)
        parts = [total] + [swap(total, axis, mask * k) for k in range(1, span)]
        mask *= span
    return parts


def on_device(
    tiles,
    tile_row,
    tile_col,
    tile_count,
    cost,
    demand,
    upper,
    col_flag,
    row_flag,
    primal_start,
    dual_start,
):
    tile = tiles.shape[1]
    total = tile_row.shape[0]
    scen = primal_start.shape[0]
    col_blocks = primal_start.shape[1] // tile
    row_blocks = dual_start.shape[1] // tile
    bf16, f32, i32 = jnp.bfloat16, jnp.float32, jnp.int32
    cost, upper, col_flag = (v.reshape(col_blocks, tile) for v in (cost, upper, col_flag))
    row_flag = row_flag.reshape(row_blocks, tile)

    small = pltpu.VMEM((scen, tile), f32)
    col_quads, row_quads = col_blocks // 4, row_blocks // 2
    col_state = pltpu.VMEM((col_quads, 2 * scen, tile), f32)
    row_state = pltpu.VMEM((row_quads, 2 * scen, tile), f32)
    row_half = pltpu.VMEM((row_quads, scen, tile), f32)
    col_terms = pltpu.VMEM((col_quads + 1, 2 * scen, tile), bf16)
    row_terms = pltpu.VMEM((row_quads + 1, 2 * scen, tile), bf16)
    tiles_like = pltpu.VMEM(tiles.shape, tiles.dtype)
    index = pltpu.SMEM((total,), i32)
    to_cols = [
        pltpu.VMEM((2, 2 * row_blocks, 2 * scen, tile), bf16),
        pltpu.VMEM((col_blocks + 1, scen, tile), f32),
    ]
    to_rows = [
        pltpu.VMEM((2, col_blocks, 2 * scen, tile), bf16),
        pltpu.VMEM((2 * row_blocks + 1, scen, tile), f32),
    ]
    turning = pl.CostEstimate(flops=0, bytes_accessed=2 * tiles.size * 2, transcendentals=0)

    keep, send, tiles, rows, cols = call(
        first_kernel,
        [tile_count, far(tile_row), far(tile_col), far(tiles), far(dual_start)],
        [SMEM_SPEC] + [FAR_SPEC] * 4,
        [col_state, col_terms, tiles_like, index, index],
        [VMEM_SPEC] * 3 + [SMEM_SPEC] * 2,
        [
            pltpu.VMEM((row_blocks, 2 * scen, tile), bf16),
            pltpu.VMEM((col_blocks + 1, scen, tile), f32),
            pltpu.VMEM(dual_start.shape, f32),
            pltpu.SemaphoreType.DMA((3 + pl.cdiv(total, PART),)),
        ],
    )
    received = swap(send, "rowblk", 1)
    terms = (keep + received[:col_quads].astype(f32)).astype(bf16)
    held_tiles, terms = lax.optimization_barrier((tiles, terms))
    parts = butterfly(terms, "rowblk", 2, 2)
    other = swap(held_tiles, "rowblk", 1)
    (turned,) = call(
        turn_kernel,
        [tile_count, tiles, terms],
        [SMEM_SPEC] + [VMEM_SPEC] * 2,
        [tiles_like],
        [VMEM_SPEC],
        [],
        turning,
    )
    (extra,) = call(
        extra_kernel,
        [dual_start, demand, row_flag, terms],
        [VMEM_SPEC] * 4,
        [pltpu.VMEM((2 * row_quads + row_blocks // 8, scen, tile), f32)],
        [VMEM_SPEC],
        [],
    )
    extra = swap(extra, "rowblk", 1)
    columns = call(
        col_kernel,
        [primal_start, cost, upper, col_flag, terms],
        [VMEM_SPEC] * 5,
        [col_state] * 3,
        [VMEM_SPEC] * 3,
        [],
    )
    start, price, limit = columns
    (grid,) = call(
        grid_kernel,
        [received, terms],
        [VMEM_SPEC] * 2,
        [pltpu.SMEM((scen, tile), i32)],
        [SMEM_SPEC],
        [pltpu.VMEM((scen, tile), i32), pltpu.SemaphoreType.DMA],
    )
    own = [tile_count, rows, cols]
    weight = jnp.ones((scen, tile), f32)
    for step in range(ITERS):
        mix = (step + 1.0) / (step + 2.0)
        last = step == ITERS - 1
        if step:
            parts = butterfly(terms, "rowblk", 2, 2)
            (other_turned,) = call(
                turn_other_kernel,
                [grid, other, terms],
                [SMEM_SPEC] + [VMEM_SPEC] * 2,
                [tiles_like],
                [VMEM_SPEC],
                [],
                turning,
            )
            vectors = [*parts, price, limit, start]
            point, weight, terms = call(
                functools.partial(primal_kernel, mix, True, len(parts)),
                [*own, turned, *vectors, other_turned, grid, weight, primal_norm, point],
                [SMEM_SPEC] * 3 + [VMEM_SPEC] * (2 + len(vectors)) + [SMEM_SPEC] + [VMEM_SPEC] * 3,
                [col_state, small, row_terms],
                [VMEM_SPEC] * 3,
                to_rows,
            )
        else:
            vectors = [*parts, price, limit, start]
            point, *half_way = call(
                functools.partial(primal_kernel, mix, False, len(parts)),
                [*own, turned, *vectors],
                [SMEM_SPEC] * 3 + [VMEM_SPEC] * (1 + len(vectors)),
                [col_state, *to_rows, small],
                [VMEM_SPEC] * 4,
                [],
            )
            (terms,) = call(
                other_kernel,
                [grid, other, *half_way],
                [SMEM_SPEC] + [VMEM_SPEC] * 4,
                [row_terms],
                [VMEM_SPEC],
                [to_rows[1]],
            )
        parts = butterfly(terms, "colblk", 4)
        if len(parts) == 4:
            parts = [parts[n] for n in (0, 2, 1, 3)]
        if step == 0:
            lines = call(
                row_kernel,
                [extra, demand, row_flag, dual_start, terms],
                [VMEM_SPEC] * 5,
                [row_state] * 3,
                [VMEM_SPEC] * 3,
                [],
            )
        vectors = [*parts, weight, *lines]
        if last:
            keep, send, terms = call(
                functools.partial(dual_kernel, mix, True, len(parts)),
                [*vectors, dual],
                [VMEM_SPEC] * (1 + len(vectors)),
                [row_half, row_half, small],
                [VMEM_SPEC] * 3,
                [],
            )
        else:
            dual, primal_norm, terms = call(
                functools.partial(dual_kernel, mix, False, len(parts)),
                [*own, grid, tiles, other, *vectors],
                [SMEM_SPEC] * 4 + [VMEM_SPEC] * (2 + len(vectors)),
                [row_state, small, col_terms],
                [VMEM_SPEC] * 3,
                to_cols,
            )
    parts = butterfly(terms, "rowblk", 4)
    (both,) = call(
        gather_kernel,
        [point, send],
        [VMEM_SPEC] * 2,
        [pltpu.VMEM((col_quads + row_quads // 2, 2 * scen, tile), f32)],
        [VMEM_SPEC],
        [],
    )
    halves = [point, keep, swap(both, "rowblk", 1)]
    shapes = [primal_start.shape, dual_start.shape]
    point, dual = call(
        result_kernel,
        halves,
        [VMEM_SPEC] * 3,
        [jax.ShapeDtypeStruct(shape, f32) for shape in shapes],
        [FAR_SPEC] * 2,
        [pltpu.VMEM(shape, f32) for shape in shapes] + [pltpu.SemaphoreType.DMA((2,))],
    )
    (weight,) = call(
        functools.partial(weight_kernel, 2.0 / lax.axis_size("rowblk")),
        [*parts, far(dual)],
        [VMEM_SPEC] * len(parts) + [FAR_SPEC],
        [jax.ShapeDtypeStruct((1, scen), f32)],
        [VMEM_SPEC],
        [],
    )
    return point, dual, weight.reshape(scen)


def solution(mesh):
    return jax.shard_map(
        on_device,
        mesh=mesh,
        in_specs=(
            P(("groups", "rowblk", "colblk"), None, None),
            P(("groups", "rowblk", "colblk")),
            P(("groups", "rowblk", "colblk")),
            P(("groups", "rowblk", "colblk")),
            P(("groups", "colblk")),
            P(None, ("groups", "rowblk")),
            P(("groups", "colblk")),
            P(("groups", "colblk")),
            P(("groups", "rowblk")),
            P(None, ("groups", "colblk")),
            P(None, ("groups", "rowblk")),
        ),
        out_specs=(P(None, ("groups", "colblk")), P(None, ("groups", "rowblk")), P("groups")),
        check_vma=False,
    )
```
